32 devices in a mesh: seq: 4 (over y, x), dp: 8 (over z, core).
Axes of the slice: x: 2, y: 2, z: 4, core: 2. Of those that a mesh axis runs over, the one named last changes fastest.
Arguments:
- queries: bfloat16 [8, 1024, 1024], P('dp', 'seq'), may hold values from -1.75 to 1.75
- keys: bfloat16 [8, 1024, 1024], P('dp', 'seq'), may hold values from -1.75 to 1.75
- values: bfloat16 [8, 1024, 1024], P('dp', 'seq'), may hold values from -6 to 6
- out_grad: bfloat16 [8, 1024, 1024], P('dp', 'seq'), may hold values from -6 to 6
- out_weight: bfloat16 [1024, 1024], P('dp'), may hold values from -0.1875 to 0.1875
- block_mask: int32 [8, 32, 8], P('dp', 'seq'), may hold values 0 or 1
Outputs:
- layer_out: bfloat16 [8, 1024, 1024], P('dp', 'seq')
- query_grad: bfloat16 [8, 1024, 1024], P('dp', 'seq')
- key_grad: bfloat16 [8, 1024, 1024], P('dp', 'seq')
- value_grad: bfloat16 [8, 1024, 1024], P('dp', 'seq')
- weight_grad: float32 [1024, 1024], P('dp')
The draws below stay inside these ranges and needn't reach their ends.
Inputs may be any that keep to these rules, and one draw needn't show every extreme that they name: `block_mask`: entries for key blocks at or after the query's own block are not read.
All inputs are finite; a program needn't handle non-finite values.
Results may differ from the reference program's by a relative error of at most 0.017.
Values may be sent and summed in bfloat16 or wider, within the bound.
A program may use at most 128 MiB of HBM per device.

```python
import jax
import jax.numpy as jnp
from jax import lax

H = 8
E = 128
DW = 1024
BLK = 32
TOK_DEV = 256
HW = 1024
BATCH = 8
LENGTH = 1024
NBLK = 8
N_SEQ = 4


def touch_ends(values, own_key, smallest, largest):
    longest = values.shape.index(max(values.shape))
    spots = []
    for shift in (0, 1):
        where = [jax.random.randint(jax.random.fold_in(own_key, axis), (), 0, length) for axis, length in enumerate(values.shape)]
        where[longest] = (where[longest] + shift) % values.shape[longest]
        spots.append(tuple(where))
    return values.at[spots[0]].set(smallest).at[spots[1]].set(largest)


def steps_of(key, extent, shards, least, top_value):
    factor_of = 1.0
    for axis_at, parts in shards:
        steps = jax.random.uniform(jax.random.fold_in(jax.random.fold_in(key, 6), axis_at), (parts,), jnp.float32, least / len(shards), top_value / len(shards))
        factor_of = factor_of * jnp.repeat(jnp.exp(steps), extent[axis_at] // parts).reshape((-1,) + (1,) * (len(extent) - 1 - axis_at))
    return factor_of


def scatter_about(own_key, shape, scale, limit, cuts=(), kind=jnp.bfloat16):
    result = jax.random.normal(own_key, shape, jnp.float32) * scale
    if len(cuts) > 0:
        result = steps_of(own_key, shape, cuts, -0.22, 0.18) * result
    return jnp.clip(result, min=-limit, max=limit).astype(kind)


def setup_inputs(seed: int = 0) -> dict:
    streams_of = jax.random.split(jax.random.key(seed), 7)
    queries = scatter_about(streams_of[0], (BATCH, LENGTH, HW), 0.3, 1.75, ((0, 8), (1, 4)))
    keys = scatter_about(streams_of[1], (BATCH, LENGTH, HW), 0.3, 1.75, ((0, 8), (1, 4)))
    values = scatter_about(streams_of[2], (BATCH, LENGTH, HW), 1.0, 6.0, ((0, 8), (1, 4)))
    out_grad = scatter_about(streams_of[3], (BATCH, LENGTH, DW), 1.0, 6.0, ((0, 8), (1, 4)))
    out_weight = scatter_about(streams_of[4], (HW, DW), HW ** -0.5, 0.1875, ((0, 8),))
    block_mask = touch_ends((jax.random.randint(streams_of[5], (BATCH, LENGTH // BLK, NBLK), 0, 2) < 1).astype(jnp.int32), jax.random.fold_in(streams_of[5], 1), 0, 1)
    return {"queries": queries, "keys": keys, "values": values, "out_grad": out_grad, "out_weight": out_weight, "block_mask": block_mask}


norm_eps = 1e-05

def visibility(block_rows):
    position = jnp.arange(TOK_DEV, dtype=jnp.int32)
    block_pos = position // BLK
    same = (block_pos[:, None] == block_pos[None, :]) & (position[None, :] <= position[:, None])
    spread = jnp.broadcast_to(block_rows[:, None, :, None], (NBLK, BLK, NBLK, BLK)).reshape(TOK_DEV, TOK_DEV)
    earlier = (block_pos[None, :] < block_pos[:, None]) & (spread == 1)
    return jnp.where(same | earlier, 1.0, 0.0).astype(jnp.float32)

def one_sequence(queries, keys, values, out_grad, out_weight, block_mask):
    f32 = jnp.float32
    bf16 = jnp.bfloat16
    q_all = queries.reshape(N_SEQ, TOK_DEV, H, E).astype(f32)
    k_all = keys.reshape(N_SEQ, TOK_DEV, H, E).astype(f32)
    v_all = values.reshape(N_SEQ, TOK_DEV, H, E).astype(f32)
    vis = jax.vmap(visibility)(block_mask.reshape(N_SEQ, NBLK, NBLK))
    scores = jnp.einsum('cthe,cshe->chts', q_all, k_all)
    weights = (scores * vis[:, None]).astype(bf16)
    states = jnp.einsum('cthe,cthf->chef', k_all, v_all).astype(bf16)
    zero_state = jnp.zeros((1, H, E, E), f32)
    prior = jnp.concatenate([zero_state, jnp.cumsum(states.astype(f32), 0)[:-1]], 0).astype(bf16)
    attn = jnp.einsum('chts,cshf->cthf', weights.astype(f32), v_all) + jnp.einsum('cthe,chef->cthf', q_all, prior.astype(f32))
    inverse = lax.rsqrt(lax.optimization_barrier(jnp.mean(attn * attn, -1, keepdims=True)) + norm_eps)
    unit = attn * inverse
    normed = unit.astype(bf16).reshape(LENGTH, HW)
    layer_out = jnp.dot(normed, out_weight, preferred_element_type=f32).astype(bf16)
    dnormed = jnp.dot(out_grad, out_weight.T, preferred_element_type=f32).reshape(N_SEQ, TOK_DEV, H, E)
    dattn = (inverse * (dnormed - unit * lax.optimization_barrier(jnp.mean(dnormed * unit, -1, keepdims=True)))).astype(bf16)
    d_all = dattn.astype(f32)
    dscore = (jnp.einsum('cthf,cshf->chts', d_all, v_all) * vis[:, None]).astype(bf16)
    back_state = jnp.einsum('cthe,cthf->chef', q_all, d_all).astype(bf16)
    back_f = back_state.astype(f32)
    later = jnp.concatenate([jnp.cumsum(back_f[::-1], 0)[:-1][::-1], zero_state], 0).astype(bf16)
    ds_f = dscore.astype(f32)
    prior_f = prior.astype(f32)
    later_f = later.astype(f32)
    query_grad = jnp.einsum('chts,cshe->cthe', ds_f, k_all) + jnp.einsum('cthf,chef->cthe', d_all, prior_f)
    key_grad = jnp.einsum('chts,cthe->cshe', ds_f, q_all) + jnp.einsum('cshf,chef->cshe', v_all, later_f)
    value_grad = jnp.einsum('chts,cthf->cshf', weights.astype(f32), d_all) + jnp.einsum('cshe,chef->cshf', k_all, later_f)
    term = jnp.dot(normed.T, out_grad, preferred_element_type=f32)
    shaped = (LENGTH, HW)
    return (layer_out, query_grad.reshape(shaped).astype(bf16), key_grad.reshape(shaped).astype(bf16), value_grad.reshape(shaped).astype(bf16), term)

def reference(queries, keys, values, out_grad, out_weight, block_mask):

    def step_fn(total, items):
        q_one, k_one, v_one, g_one, m_one = items
        layer_out, query_grad, key_grad, value_grad, term = one_sequence(q_one, k_one, v_one, g_one, out_weight, m_one)
        return (total + term, (layer_out, query_grad, key_grad, value_grad))
    start = jnp.zeros((HW, DW), jnp.float32)
    total, outs = lax.scan(step_fn, start, (queries, keys, values, out_grad, block_mask))
    weight_grad = total * (1.0 / jnp.sqrt(jnp.float32(BATCH * LENGTH)))
    return (outs[0], outs[1], outs[2], outs[3], weight_grad)
```

```python
import functools
import math

import jax
import jax.numpy as jnp
from jax import lax
from jax.experimental import pallas as pl
from jax.experimental.pallas import tpu as pltpu
from jax.sharding import PartitionSpec as P

H = 8
norm_eps = 1e-05
MESH = pl.DeviceIdType.MESH
f32 = jnp.float32
bf16 = jnp.bfloat16
QUAD = 4
CHUNKS = 4
UNROLL = 4


def bit(i, m):
    return lax.rem(lax.div(i, m), 2)


def flip(i, m):
    return i + m - 2 * m * bit(i, m)


def mm(a, b, da, db):
    return lax.dot_general(a, b, (((da,), (db,)), ((), ())), preferred_element_type=f32)


def over_heads(lo, hi, fn):
    if hi <= lo:
        return

    def body(h, c):
        fn(h)
        return c

    lax.fori_loop(lo, hi, body, 0, unroll=UNROLL)


def visibility(mask, tokens):
    blocks = mask.shape[0]
    width = tokens // blocks
    t = lax.broadcasted_iota(jnp.int32, (tokens, blocks), 0)
    b = lax.broadcasted_iota(jnp.int32, (tokens, blocks), 1) * width
    member = jnp.where((t >= b) & (t < b + width), 1.0, 0.0)
    r = lax.broadcasted_iota(jnp.int32, (blocks, blocks), 0)
    c = lax.broadcasted_iota(jnp.int32, (blocks, blocks), 1)
    lower = jnp.where((mask == 1) & (c < r), 1.0, 0.0)
    member = member.astype(bf16)
    rows = mm(member, lower.astype(bf16), 1, 0).astype(bf16)
    earlier = mm(rows, member, 1, 1)
    same = mm(member, member, 1, 1)
    row = lax.broadcasted_iota(jnp.int32, (tokens, tokens), 0)
    col = lax.broadcasted_iota(jnp.int32, (tokens, tokens), 1)
    return earlier + jnp.where(col <= row, same, 0.0)


def kernel(
    n_seq, n_dp, q_hbm, k_hbm, v_hbm, g_hbm, w_ref, mask_hbm,
    out_ref, qg_ref, kg_ref, vg_ref, wg_ref,
    w_full, vis_ref, s_out, s_in, acc, prior, later, wts, attn, inv, normed,
    dnormed, dattn, dsc, term, a_in, u_out, x_in, z_out, z_in, z_own, r_out, r_in, f_out,
    w1_s, w1_r, w2_s, w2_r, w3_s, w3_r, st_s, st_r, a_s, a_r, x_s, x_r, z_s, z_r, r_s, r_r,
    f_s, f_r, q_ref, k_ref, v_ref, g_ref, mask_ref, in_s,
):
    tokens, width = q_ref.shape
    size = width // H
    n_z = n_dp // 2
    rows = w_ref.shape[0]
    cols = w_ref.shape[1]
    quarter = cols // QUAD
    n_bits = n_seq.bit_length() - 1
    s = lax.axis_index("seq")
    d = lax.axis_index("dp")
    z = lax.div(d, 2)
    core = lax.rem(d, 2)
    s4 = lax.rem(s, QUAD)
    peer = flip(d, 1)
    seq_peer = {j: s for j in (1, 2, 3)}
    seq_peer[1] = flip(s, 1)
    seq_peer[2] = flip(s, 2)
    seq_peer[3] = flip(flip(s, 1), 2)

    def qcols(seq_index):
        return pl.ds(pl.multiple_of(lax.rem(seq_index, QUAD) * quarter, quarter), quarter)

    def brow(dp_index):
        return pl.ds(pl.multiple_of(dp_index * rows, rows), rows)

    def hcols(h):
        return pl.ds(pl.multiple_of(h * size, size), size)

    def up(k):
        return lax.rem(z + k, n_z)

    def down(k):
        return lax.rem(z + n_z - k, n_z)

    def rc(src, dst, ss, rs, dev):
        return pltpu.make_async_remote_copy(
            src_ref=src, dst_ref=dst, send_sem=ss, recv_sem=rs, device_id=dev,
            device_id_type=MESH,
        )

    sent = []

    def go(*a):
        c = rc(*a)
        c.start()
        sent.append(c)

    def arrive(dst, ss, rs, dev):
        rc(dst, dst, ss, rs, dev).wait_recv()

    loads = {}
    pairs = [(k_hbm, k_ref), (v_hbm, v_ref), (q_hbm, q_ref), (mask_hbm, mask_ref), (g_hbm, g_ref)]
    pairs.append((w_ref, w_full.at[brow(d)]))
    for i, name in enumerate("kvqmgw"):
        loads[name] = pltpu.make_async_copy(pairs[i][0], pairs[i][1], in_s.at[i])
        loads[name].start()

    barrier = pltpu.get_barrier_semaphore()
    partners = [(s, peer)]
    partners += [(seq_peer[j], d) for j in (1, 2, 3)]
    partners += [(flip(s, 1 << b), d) for b in range(2, n_bits)]
    partners += [(s, up(i) * 2 + core) for i in range(1, n_z)]
    for p in partners:
        pl.semaphore_signal(barrier, inc=1, device_id=p, device_id_type=MESH)
    pl.semaphore_wait(barrier, len(partners))

    own_q = [qcols(s), qcols(seq_peer[3])]
    for part in range(2):
        for i in range(1, n_z):
            go(
                w_ref.at[:, own_q[part]], w_full.at[brow(d), own_q[part]],
                w1_s.at[part, i - 1], w1_r.at[part, i - 1], (s, up(i) * 2 + core),
            )
    go(w_ref, w_full.at[brow(d)], w3_s.at[0], w3_r.at[0], (s, peer))
    loads["k"].wait()
    loads["v"].wait()

    half = width // CHUNKS

    def chunk(c):
        return pl.ds(c * half, half)

    def send_state(way, b, c):
        go(
            s_out.at[way, b, chunk(c)], s_in.at[way, b, chunk(c)],
            st_s.at[way, b, c], st_r.at[way, b, c], (flip(s, 1 << b), d),
        )

    def state_step(way, b, c):
        arrive(s_in.at[way, b, chunk(c)], st_s.at[way, b, c], st_r.at[way, b, c], (flip(s, 1 << b), d))
        got = s_in[way, b, chunk(c)].astype(f32)
        if b + 1 < n_bits:
            s_out[way, b + 1, chunk(c)] = (s_out[way, b, chunk(c)].astype(f32) + got).astype(bf16)
            send_state(way, b + 1, c)
        own_bit = bit(s, 1 << b)
        use = (own_bit if way == 0 else 1 - own_bit).astype(f32)
        if b == 0:
            acc[chunk(c)] = got * use
        else:
            acc[chunk(c)] += got * use

    per = H // CHUNKS
    for c in range(CHUNKS):

        def make_state(h):
            st = mm(k_ref[:, hcols(h)], v_ref[:, hcols(h)], 0, 0)
            s_out[0, 0, hcols(h)] = st.astype(bf16)

        over_heads(c * per, (c + 1) * per, make_state)
        send_state(0, 0, c)

    loads["q"].wait()
    loads["m"].wait()
    vis_ref[...] = visibility(mask_ref[...], tokens)

    def local_attn(h):
        sc = mm(q_ref[:, hcols(h)], k_ref[:, hcols(h)], 1, 1)
        wt = (sc * vis_ref[...]).astype(bf16)
        wts[h] = wt
        attn[:, hcols(h)] = mm(wt, v_ref[:, hcols(h)], 1, 0)

    over_heads(0, H, local_attn)

    for c in range(CHUNKS):
        state_step(0, 0, c)

    for i in range(1, n_z):
        src = down(i) * 2 + core
        arrive(w_full.at[brow(src), own_q[0]], w1_s.at[0, i - 1], w1_r.at[0, i - 1], (s, src))
        for j in (1, 2):
            go(
                w_full.at[brow(src), own_q[0]], w_full.at[brow(src), own_q[0]],
                w2_s.at[j - 1, i - 1], w2_r.at[j - 1, i - 1], (seq_peer[j], d),
            )

    for b in range(1, n_bits):
        for c in range(CHUNKS):
            state_step(0, b, c)
    prior[...] = acc[...].astype(bf16)

    loads["g"].wait()
    loads["w"].wait()

    def finish_attn(h):
        a = attn[:, hcols(h)] + mm(q_ref[:, hcols(h)], prior[hcols(h), :], 1, 0)
        iv = lax.rsqrt(jnp.mean(a * a, -1, keepdims=True) + norm_eps)
        u = a * iv
        attn[:, hcols(h)] = u
        inv[h] = iv
        n = u.astype(bf16)
        normed[:, hcols(h)] = n
        term[hcols(h), :] = mm(n, g_ref[...], 0, 0).astype(bf16)

    over_heads(0, H, finish_attn)

    for i in range(n_z):
        zz = up(i + 1)
        go(
            term.at[brow(zz * 2 + 1 - core)], a_in.at[zz], a_s.at[i], a_r.at[i], (s, peer)
        )

    for i in range(1, n_z):
        src = down(i) * 2 + core
        arrive(w_full.at[brow(src), own_q[1]], w1_s.at[1, i - 1], w1_r.at[1, i - 1], (s, src))
        for j in (1, 2):
            arrive(
                w_full.at[brow(src), qcols(seq_peer[j])], w2_s.at[j - 1, i - 1],
                w2_r.at[j - 1, i - 1], (seq_peer[j], d),
            )
        go(w_full.at[brow(src)], w_full.at[brow(src)], w3_s.at[i], w3_r.at[i], (s, peer))

    for i in range(n_z):
        zz = up(i + 1)
        arrive(a_in.at[zz], a_s.at[i], a_r.at[i], (s, peer))
        u_out[zz] = (term[brow(zz * 2 + core), :].astype(f32) + a_in[zz].astype(f32)).astype(bf16)
        for j in (1, 2, 3):
            go(
                u_out.at[zz, :, qcols(seq_peer[j])], x_in.at[j - 1, zz],
                x_s.at[j - 1, i], x_r.at[j - 1, i], (seq_peer[j], d),
            )

    for i in range(n_z):
        src = down(i) * 2 + 1 - core
        arrive(w_full.at[brow(src)], w3_s.at[i], w3_r.at[i], (s, peer))

    def grad_norm(h):
        dn = mm(g_ref[...], w_full[hcols(h), :], 1, 1)
        u = attn[:, hcols(h)]
        da = (inv[h] * (dn - u * jnp.mean(dn * u, -1, keepdims=True))).astype(bf16)
        dattn[:, hcols(h)] = da
        s_out[1, 0, hcols(h)] = mm(q_ref[:, hcols(h)], da, 0, 0).astype(bf16)

    for c in range(CHUNKS):
        over_heads(c * per, (c + 1) * per, grad_norm)
        send_state(1, 0, c)

    def z_step(i):
        zz = up(i + 1)
        total = u_out[zz, :, qcols(s)].astype(f32)
        for j in (1, 2, 3):
            arrive(x_in.at[j - 1, zz], x_s.at[j - 1, i], x_r.at[j - 1, i], (seq_peer[j], d))
            total = total + x_in[j - 1, zz].astype(f32)
        if i < n_z - 1:
            z_out[i] = total.astype(bf16)
            go(z_out.at[i], z_in.at[i], z_s.at[i], z_r.at[i], (s, zz * 2 + core))
        else:
            z_own[...] = total

    def make_scores(h):
        ds = (mm(dattn[:, hcols(h)], v_ref[:, hcols(h)], 1, 1) * vis_ref[...]).astype(bf16)
        dsc[h] = ds
        qg = mm(ds, k_ref[:, hcols(h)], 1, 0) + mm(dattn[:, hcols(h)], prior[hcols(h), :], 1, 1)
        qg_ref[:, hcols(h)] = qg.astype(bf16)
        out_ref[:, hcols(h)] = mm(normed[...], w_full[:, hcols(h)], 1, 0).astype(bf16)

    for i in range(n_z):
        over_heads(i * H // n_z, (i + 1) * H // n_z, make_scores)
        z_step(i)

    for c in range(CHUNKS):
        state_step(1, 0, c)

    def local_grads(h):
        attn[:, hcols(h)] = mm(dsc[h], q_ref[:, hcols(h)], 0, 0)
        dnormed[:, hcols(h)] = mm(wts[h], dattn[:, hcols(h)], 0, 0)

    over_heads(0, H, local_grads)

    total = z_own[...]
    for i in range(n_z - 1):
        src = down(i + 1) * 2 + core
        arrive(z_in.at[i], z_s.at[i], z_r.at[i], (s, src))
        total = total + z_in[i].astype(f32)
    for b in range(2, n_bits):
        r_out[b - 2] = total.astype(bf16)
        dev = (flip(s, 1 << b), d)
        go(r_out.at[b - 2], r_in.at[b - 2], r_s.at[b - 2], r_r.at[b - 2], dev)
        arrive(r_in.at[b - 2], r_s.at[b - 2], r_r.at[b - 2], dev)
        total = total + r_in[b - 2].astype(f32)
    f_out[:, qcols(s)] = total.astype(bf16)
    for j in (1, 2, 3):
        go(
            f_out.at[:, qcols(s)], f_out.at[:, qcols(s)], f_s.at[j - 1], f_r.at[j - 1],
            (seq_peer[j], d),
        )

    for b in range(1, n_bits):
        for c in range(CHUNKS):
            state_step(1, b, c)
    later[...] = acc[...].astype(bf16)

    def last_grads(h):
        kg = attn[:, hcols(h)] + mm(v_ref[:, hcols(h)], later[hcols(h), :], 1, 1)
        kg_ref[:, hcols(h)] = kg.astype(bf16)
        vg = dnormed[:, hcols(h)] + mm(k_ref[:, hcols(h)], later[hcols(h), :], 1, 0)
        vg_ref[:, hcols(h)] = vg.astype(bf16)

    over_heads(0, H, last_grads)

    for j in (1, 2, 3):
        arrive(f_out.at[:, qcols(seq_peer[j])], f_s.at[j - 1], f_r.at[j - 1], (seq_peer[j], d))
    wg_ref[...] = f_out[...].astype(f32) * (1.0 / math.sqrt(n_seq * n_dp * tokens))
    for c in sent:
        c.wait_send()


def store(*refs):
    src, dst, sems = refs[:5], refs[5:10], refs[10]
    saves = [pltpu.make_async_copy(src[i], dst[i], sems.at[i]) for i in range(5)]
    for c in saves:
        c.start()
    for c in saves:
        c.wait()


def on_device(n_seq, n_dp, queries, keys, values, out_grad, out_weight, block_mask):
    _, tokens, width = queries.shape
    rows, cols = out_weight.shape
    size = width // H
    n_z = n_dp // 2
    n_bits = n_seq.bit_length() - 1
    more = max(n_bits - 2, 1)
    quarter = cols // QUAD
    dma = pltpu.SemaphoreType.DMA
    vm = pltpu.VMEM
    act = jax.ShapeDtypeStruct((tokens, width), bf16)
    spec = pl.BlockSpec(memory_space=pltpu.VMEM)
    outs = pl.pallas_call(
        functools.partial(kernel, n_seq, n_dp),
        out_shape=[vm((tokens, width), bf16)] * 4 + [vm((rows, cols), f32)],
        in_specs=[pl.BlockSpec(memory_space=pltpu.HBM)] * 6,
        out_specs=[spec] * 5,
        scratch_shapes=[
            vm((width, cols), bf16),
            vm((tokens, tokens), f32),
            vm((2, n_bits, width, size), bf16),
            vm((2, n_bits, width, size), bf16),
            vm((width, size), f32),
            vm((width, size), bf16),
            vm((width, size), bf16),
            vm((H, tokens, tokens), bf16),
            vm((tokens, width), f32),
            vm((H, tokens, 1), f32),
            vm((tokens, width), bf16),
            vm((tokens, width), f32),
            vm((tokens, width), bf16),
            vm((H, tokens, tokens), bf16),
            vm((width, cols), bf16),
            vm((n_z, rows, cols), bf16),
            vm((n_z, rows, cols), bf16),
            vm((3, n_z, rows, quarter), bf16),
            vm((n_z - 1, rows, quarter), bf16),
            vm((n_z - 1, rows, quarter), bf16),
            vm((rows, quarter), f32),
            vm((more, rows, quarter), bf16),
            vm((more, rows, quarter), bf16),
            vm((rows, cols), bf16),
            dma((2, n_z - 1)), dma((2, n_z - 1)),
            dma((2, n_z - 1)), dma((2, n_z - 1)),
            dma((n_z,)), dma((n_z,)),
            dma((2, n_bits, CHUNKS)), dma((2, n_bits, CHUNKS)),
            dma((n_z,)), dma((n_z,)),
            dma((3, n_z)), dma((3, n_z)),
            dma((n_z - 1,)), dma((n_z - 1,)),
            dma((more,)), dma((more,)),
            dma((3,)), dma((3,)),
            vm((tokens, width), bf16), vm((tokens, width), bf16),
            vm((tokens, width), bf16), vm((tokens, width), bf16),
            vm(block_mask.shape[1:], jnp.int32), dma((6,)),
        ],
        compiler_params=pltpu.CompilerParams(
            collective_id=0, has_side_effects=True, vmem_limit_bytes=40 * 1024 * 1024
        ),
    )(*[pltpu.with_memory_space_constraint(a, pltpu.HBM) for a in (queries[0], keys[0], values[0], out_grad[0], out_weight, block_mask[0])])
    outs = pl.pallas_call(
        store,
        out_shape=[jax.ShapeDtypeStruct(o.shape, o.dtype) for o in outs],
        in_specs=[spec] * 5,
        out_specs=[pl.BlockSpec(memory_space=pltpu.HBM)] * 5,
        scratch_shapes=[dma((5,))],
        compiler_params=pltpu.CompilerParams(vmem_limit_bytes=4 * 1024 * 1024),
    )(*outs)
    return tuple(o[None] for o in outs[:4]) + (outs[4],)


def solution(mesh):
    token_spec = P("dp", "seq", None)
    row_spec = P("dp", None)
    return jax.shard_map(
        functools.partial(on_device, mesh.shape["seq"], mesh.shape["dp"]),
        mesh=mesh,
        in_specs=(token_spec,) * 4 + (row_spec, token_spec),
        out_specs=(token_spec,) * 4 + (row_spec,),
        check_vma=False,
    )
```

```python
import functools
import math

import jax
import jax.numpy as jnp
from jax import lax
from jax.experimental import pallas as pl
from jax.experimental.pallas import tpu as pltpu
from jax.sharding import PartitionSpec as P

H = 8
norm_eps = 1e-05
MESH = pl.DeviceIdType.MESH
f32 = jnp.float32
bf16 = jnp.bfloat16
QUAD = 4
CHUNKS = 4
UNROLL = 4


def bit(i, m):
    return lax.rem(lax.div(i, m), 2)


def flip(i, m):
    return i + m - 2 * m * bit(i, m)


def mm(a, b, da, db):
    return lax.dot_general(a, b, (((da,), (db,)), ((), ())), preferred_element_type=f32)


def over_heads(first, count, fn):
    def body(i, c):
        fn(first + i)
        return c

    lax.fori_loop(0, count, body, 0, unroll=min(UNROLL, count))


def visibility(mask, tokens):
    blocks = mask.shape[0]
    width = tokens // blocks
    t = lax.broadcasted_iota(jnp.int32, (tokens, blocks), 0)
    b = lax.broadcasted_iota(jnp.int32, (tokens, blocks), 1) * width
    member = jnp.where((t >= b) & (t < b + width), 1.0, 0.0)
    r = lax.broadcasted_iota(jnp.int32, (blocks, blocks), 0)
    c = lax.broadcasted_iota(jnp.int32, (blocks, blocks), 1)
    lower = jnp.where((mask == 1) & (c < r), 1.0, 0.0)
    member = member.astype(bf16)
    rows = mm(member, lower.astype(bf16), 1, 0).astype(bf16)
    earlier = mm(rows, member, 1, 1)
    same = mm(member, member, 1, 1)
    row = lax.broadcasted_iota(jnp.int32, (tokens, tokens), 0)
    col = lax.broadcasted_iota(jnp.int32, (tokens, tokens), 1)
    return earlier + jnp.where(col <= row, same, 0.0)


def kernel(
    n_seq, n_dp, q_hbm, k_hbm, v_hbm, g_hbm, w_ref, mask_hbm,
    out_ref, qg_ref, kg_ref, vg_ref, wg_ref,
    w_full, vis_ref, s_out, s_in, acc, prior, later, wts, attn, inv, normed,
    dnormed, dattn, dsc, term, a_in, u_out, first_in, mid_out, second_in, z_out, z_in, z_own,
    r_out, r_in, f_all,
    w1_s, w1_r, w2_s, w2_r, w3_s, w3_r, st_s, st_r, a_s, a_r, x_s, x_r, z_s, z_r, r_s, r_r,
    f_s, f_r, q_ref, k_ref, v_ref, g_ref, mask_ref, in_s,
):
    tokens, width = q_ref.shape
    size = width // H
    n_z = n_dp // 2
    rows = w_ref.shape[0]
    cols = w_ref.shape[1]
    quarter = cols // QUAD
    eighth = quarter // 2
    n_bits = n_seq.bit_length() - 1
    s = lax.axis_index("seq")
    d = lax.axis_index("dp")
    z = lax.div(d, 2)
    core = lax.rem(d, 2)
    peer = flip(d, 1)
    seq_peer = {1: flip(s, 1), 2: flip(s, 2), 3: flip(flip(s, 1), 2)}
    bits = (bit(s, 1), bit(s, 2))
    zb = n_z // CHUNKS
    half = width // CHUNKS
    per = H // CHUNKS

    def qcols(seq_index):
        return pl.ds(pl.multiple_of(lax.rem(seq_index, QUAD) * quarter, quarter), quarter)

    def brow(dp_index):
        return pl.ds(pl.multiple_of(dp_index * rows, rows), rows)

    def hcols(h):
        return pl.ds(pl.multiple_of(h * size, size), size)

    def up(k):
        return lax.rem(z + k, n_z)

    def down(k):
        return lax.rem(z + n_z - k, n_z)

    def chunk_at(i):
        return lax.rem(lax.div(z, zb) + 1 + i, CHUNKS)

    def chunk(i):
        return pl.ds(pl.multiple_of(chunk_at(i) * half, half), half)

    def heads_of(i, fn):
        over_heads(chunk_at(i) * per, per, fn)

    def rc(src, dst, ss, rs, dev):
        return pltpu.make_async_remote_copy(
            src_ref=src, dst_ref=dst, send_sem=ss, recv_sem=rs, device_id=dev,
            device_id_type=MESH,
        )

    sent = []

    def go(*a, when=None):
        c = rc(*a)
        if when is None:
            c.start()
        else:
            pl.when(when)(c.start)
        sent.append((c, when))

    def arrive(dst, ss, rs, dev):
        rc(dst, dst, ss, rs, dev).wait_recv()

    loads = {}
    pairs = [(k_hbm, k_ref), (v_hbm, v_ref), (q_hbm, q_ref), (mask_hbm, mask_ref), (g_hbm, g_ref)]
    pairs.append((w_ref, w_full.at[brow(d)]))
    for i, name in enumerate("kvqmgw"):
        loads[name] = pltpu.make_async_copy(pairs[i][0], pairs[i][1], in_s.at[i])
        loads[name].start()

    barrier = pltpu.get_barrier_semaphore()
    partners = [(s, peer)]
    partners += [(seq_peer[j], d) for j in (1, 2, 3)]
    partners += [(flip(s, 1 << b), d) for b in range(2, n_bits)]
    partners += [(s, up(i) * 2 + core) for i in range(1, n_z)]
    for p in partners:
        pl.semaphore_signal(barrier, inc=1, device_id=p, device_id_type=MESH)
    acc[...] = jnp.zeros_like(acc)
    pl.semaphore_wait(barrier, len(partners))

    own_q = [qcols(s), qcols(seq_peer[3])]
    for part in range(2):
        for i in range(1, n_z):
            go(
                w_ref.at[:, own_q[part]], w_full.at[brow(d), own_q[part]],
                w1_s.at[part, i - 1], w1_r.at[part, i - 1], (s, up(i) * 2 + core),
            )
    go(w_ref, w_full.at[brow(d)], w3_s.at[0], w3_r.at[0], (s, peer))
    loads["k"].wait()
    loads["v"].wait()

    def roles(way, b):
        own = bit(s, 1 << b)
        above = lax.div(s, 2 << b)
        last = (n_seq >> (b + 1)) - 1
        takes = own == 1 if way == 0 else own == 0
        if last == 0:
            return takes, None
        return takes, above != last if way == 0 else above != 0

    def send_state(way, b, i, when):
        go(
            s_out.at[way, b, chunk(i)], s_in.at[way, b, chunk(i)],
            st_s.at[way, b, i], st_r.at[way, b, i], (flip(s, 1 << b), d), when=when,
        )

    def first_state(way, i):
        takes, more = roles(way, 0)
        gives = jnp.logical_not(takes)
        send_state(way, 0, i, gives if more is None else jnp.logical_or(gives, more))

    def state_step(way, b, i):
        takes, more = roles(way, b)

        def receive():
            arrive(
                s_in.at[way, b, chunk(i)], st_s.at[way, b, i], st_r.at[way, b, i],
                (flip(s, 1 << b), d),
            )

        def pass_on():
            total = s_out[way, b, chunk(i)].astype(f32) + s_in[way, b, chunk(i)].astype(f32)
            s_out[way, b + 1, chunk(i)] = total.astype(bf16)

        def take():
            acc[chunk(i)] += s_in[way, b, chunk(i)].astype(f32)

        if more is None:
            pl.when(takes)(receive)
        else:
            pl.when(jnp.logical_or(takes, more))(receive)
            pl.when(more)(pass_on)
            send_state(way, b + 1, i, more)
        pl.when(takes)(take)

    def make_state(h):
        st = mm(k_ref[:, hcols(h)], v_ref[:, hcols(h)], 0, 0)
        s_out[0, 0, hcols(h)] = st.astype(bf16)

    for i in range(CHUNKS):
        heads_of(i, make_state)
        first_state(0, i)

    loads["q"].wait()
    loads["m"].wait()
    vis_ref[...] = visibility(mask_ref[...], tokens)

    def local_attn(h):
        sc = mm(q_ref[:, hcols(h)], k_ref[:, hcols(h)], 1, 1)
        wt = (sc * vis_ref[...]).astype(bf16)
        wts[h] = wt
        attn[:, hcols(h)] = mm(wt, v_ref[:, hcols(h)], 1, 0)

    for i in range(CHUNKS):
        heads_of(i, local_attn)

    for i in range(CHUNKS):
        state_step(0, 0, i)

    for i in range(1, n_z):
        src = down(i) * 2 + core
        arrive(w_full.at[brow(src), own_q[0]], w1_s.at[0, i - 1], w1_r.at[0, i - 1], (s, src))
        for j in (1, 2):
            go(
                w_full.at[brow(src), own_q[0]], w_full.at[brow(src), own_q[0]],
                w2_s.at[j - 1, i - 1], w2_r.at[j - 1, i - 1], (seq_peer[j], d),
            )

    loads["g"].wait()
    loads["w"].wait()

    def finish_attn(h):
        a = attn[:, hcols(h)] + mm(q_ref[:, hcols(h)], prior[hcols(h), :], 1, 0)
        iv = lax.rsqrt(jnp.mean(a * a, -1, keepdims=True) + norm_eps)
        u = a * iv
        attn[:, hcols(h)] = u
        inv[h] = iv
        n = u.astype(bf16)
        normed[:, hcols(h)] = n
        term[hcols(h), :] = mm(n, g_ref[...], 0, 0).astype(bf16)

    def sub(side, i0, i1):
        return 2 * quarter * side + i0 * quarter + i1 * eighth

    def lanes(start, length):
        return pl.ds(pl.multiple_of(start, eighth), length)

    def swap_cores(i):
        zz = up(i + 1)
        go(term.at[brow(zz * 2 + 1 - core)], a_in.at[i], a_s.at[i], a_r.at[i], (s, peer))

    def first_cut(i):
        zz = up(i + 1)
        arrive(a_in.at[i], a_s.at[i], a_r.at[i], (s, peer))
        u_out[i] = (term[brow(zz * 2 + core), :].astype(f32) + a_in[i].astype(f32)).astype(bf16)
        for side in (0, 1):
            go(
                u_out.at[i, :, lanes(sub(side, 1 - bits[side], 0), quarter)], first_in.at[side, i],
                x_s.at[0, side, i], x_r.at[0, side, i], (seq_peer[1 + side], d),
            )

    def second_cut(i):
        for side in (0, 1):
            arrive(first_in.at[side, i], x_s.at[0, side, i], x_r.at[0, side, i], (seq_peer[1 + side], d))
            other = 1 - bits[1 - side]
            got = first_in[side, i, :, lanes(other * eighth, eighth)].astype(f32)
            own = u_out[i, :, lanes(sub(side, bits[side], other), eighth)].astype(f32)
            mid_out[side, i] = (own + got).astype(bf16)
            go(
                mid_out.at[side, i], second_in.at[side, i],
                x_s.at[1, side, i], x_r.at[1, side, i], (seq_peer[2 - side], d),
            )

    def z_step(i):
        zz = up(i + 1)
        for side in (0, 1):
            arrive(second_in.at[side, i], x_s.at[1, side, i], x_r.at[1, side, i], (seq_peer[2 - side], d))
            mine = bits[1 - side]
            total = u_out[i, :, lanes(sub(side, bits[side], mine), eighth)].astype(f32)
            total = total + first_in[side, i, :, lanes(mine * eighth, eighth)].astype(f32)
            total = total + second_in[side, i].astype(f32)
            if i < n_z - 1:
                z_out[i, :, side * eighth:(side + 1) * eighth] = total.astype(bf16)
            else:
                z_own[:, side * eighth:(side + 1) * eighth] = total
        if i < n_z - 1:
            go(z_out.at[i], z_in.at[i], z_s.at[i], z_r.at[i], (s, zz * 2 + core))

    def blocks_at(i):
        if zb == 1:
            return [i]
        return list(range(n_z)) if i == CHUNKS - 1 else []

    for i in range(CHUNKS):
        for b in range(1, n_bits):
            state_step(0, b, i)
        prior[chunk(i)] = acc[chunk(i)].astype(bf16)
        acc[chunk(i)] = jnp.zeros((half, size), f32)
        heads_of(i, finish_attn)
        for j in blocks_at(i):
            swap_cores(j)
        if i >= 1:
            for j in blocks_at(i - 1):
                first_cut(j)

    for i in range(1, n_z):
        src = down(i) * 2 + core
        arrive(w_full.at[brow(src), own_q[1]], w1_s.at[1, i - 1], w1_r.at[1, i - 1], (s, src))
        for j in (1, 2):
            arrive(
                w_full.at[brow(src), qcols(seq_peer[j])], w2_s.at[j - 1, i - 1],
                w2_r.at[j - 1, i - 1], (seq_peer[j], d),
            )
        go(w_full.at[brow(src)], w_full.at[brow(src)], w3_s.at[i], w3_r.at[i], (s, peer))

    for j in blocks_at(CHUNKS - 1):
        first_cut(j)

    def grad_norm(h):
        dn = mm(g_ref[...], w_full[hcols(h), :], 1, 1)
        u = attn[:, hcols(h)]
        da = (inv[h] * (dn - u * jnp.mean(dn * u, -1, keepdims=True))).astype(bf16)
        dattn[:, hcols(h)] = da
        s_out[1, 0, hcols(h)] = mm(q_ref[:, hcols(h)], da, 0, 0).astype(bf16)

    def parts(i):
        return range(i * n_z // CHUNKS, (i + 1) * n_z // CHUNKS)

    for i in range(CHUNKS):
        for j in parts(i):
            second_cut(j)
        if i == 0:
            for j in range(n_z):
                src = down(j) * 2 + 1 - core
                arrive(w_full.at[brow(src)], w3_s.at[j], w3_r.at[j], (s, peer))
        heads_of(i, grad_norm)
        first_state(1, i)

    def make_scores(h):
        ds = (mm(dattn[:, hcols(h)], v_ref[:, hcols(h)], 1, 1) * vis_ref[...]).astype(bf16)
        dsc[h] = ds
        qg = mm(ds, k_ref[:, hcols(h)], 1, 0) + mm(dattn[:, hcols(h)], prior[hcols(h), :], 1, 1)
        qg_ref[:, hcols(h)] = qg.astype(bf16)
        out_ref[:, hcols(h)] = mm(normed[...], w_full[:, hcols(h)], 1, 0).astype(bf16)

    for i in range(CHUNKS):
        heads_of(i, make_scores)
        for j in parts(i):
            z_step(j)
        state_step(1, 0, i)

    def local_grads(h):
        attn[:, hcols(h)] = mm(dsc[h], q_ref[:, hcols(h)], 0, 0)
        dnormed[:, hcols(h)] = mm(wts[h], dattn[:, hcols(h)], 0, 0)

    for i in range(CHUNKS):
        heads_of(i, local_grads)

    total = z_own[...]
    for i in range(n_z - 1):
        src = down(i + 1) * 2 + core
        arrive(z_in.at[i], z_s.at[i], z_r.at[i], (s, src))
        total = total + z_in[i].astype(f32)
    for b in range(2, n_bits):
        own = total.astype(bf16)
        r_out[b - 2] = own
        dev = (flip(s, 1 << b), d)
        go(r_out.at[b - 2], r_in.at[b - 2], r_s.at[b - 2], r_r.at[b - 2], dev)
        arrive(r_in.at[b - 2], r_s.at[b - 2], r_r.at[b - 2], dev)
        total = own.astype(f32) + r_in[b - 2].astype(f32)
    place = lax.rem(s, QUAD)
    f_all[place] = total.astype(bf16)
    for j in (1, 2, 3):
        go(f_all.at[place], f_all.at[place], f_s.at[j - 1], f_r.at[j - 1], (seq_peer[j], d))

    def last_grads(h):
        kg = attn[:, hcols(h)] + mm(v_ref[:, hcols(h)], later[hcols(h), :], 1, 1)
        kg_ref[:, hcols(h)] = kg.astype(bf16)
        vg = dnormed[:, hcols(h)] + mm(k_ref[:, hcols(h)], later[hcols(h), :], 1, 0)
        vg_ref[:, hcols(h)] = vg.astype(bf16)

    for i in range(CHUNKS):
        for b in range(1, n_bits):
            state_step(1, b, i)
        later[chunk(i)] = acc[chunk(i)].astype(bf16)
        heads_of(i, last_grads)

    for j in (1, 2, 3):
        there = lax.rem(seq_peer[j], QUAD)
        arrive(f_all.at[there], f_s.at[j - 1], f_r.at[j - 1], (seq_peer[j], d))
    scale = 1.0 / math.sqrt(n_seq * n_dp * tokens)
    for p in range(QUAD):
        xy = (p % 2, p // 2)
        for side in (0, 1):
            at = sub(side, xy[side], xy[1 - side])
            got = f_all[p, :, side * eighth:(side + 1) * eighth]
            wg_ref[:, at:at + eighth] = got.astype(f32) * scale
    for c, when in sent:
        if when is None:
            c.wait_send()
        else:
            pl.when(when)(c.wait_send)


def store(*refs):
    src, dst, sems = refs[:5], refs[5:10], refs[10]
    saves = [pltpu.make_async_copy(src[i], dst[i], sems.at[i]) for i in range(5)]
    for c in saves:
        c.start()
    for c in saves:
        c.wait()


def on_device(n_seq, n_dp, queries, keys, values, out_grad, out_weight, block_mask):
    _, tokens, width = queries.shape
    rows, cols = out_weight.shape
    size = width // H
    n_z = n_dp // 2
    n_bits = n_seq.bit_length() - 1
    more = max(n_bits - 2, 1)
    quarter = cols // QUAD
    eighth = quarter // 2
    dma = pltpu.SemaphoreType.DMA
    vm = pltpu.VMEM
    act = jax.ShapeDtypeStruct((tokens, width), bf16)
    spec = pl.BlockSpec(memory_space=pltpu.VMEM)
    outs = pl.pallas_call(
        functools.partial(kernel, n_seq, n_dp),
        out_shape=[vm((tokens, width), bf16)] * 4 + [vm((rows, cols), f32)],
        in_specs=[pl.BlockSpec(memory_space=pltpu.HBM)] * 6,
        out_specs=[spec] * 5,
        scratch_shapes=[
            vm((width, cols), bf16),
            vm((tokens, tokens), f32),
            vm((2, n_bits, width, size), bf16),
            vm((2, n_bits, width, size), bf16),
            vm((width, size), f32),
            vm((width, size), bf16),
            vm((width, size), bf16),
            vm((H, tokens, tokens), bf16),
            vm((tokens, width), f32),
            vm((H, tokens, 1), f32),
            vm((tokens, width), bf16),
            vm((tokens, width), f32),
            vm((tokens, width), bf16),
            vm((H, tokens, tokens), bf16),
            vm((width, cols), bf16),
            vm((n_z, rows, cols), bf16),
            vm((n_z, rows, cols), bf16),
            vm((2, n_z, rows, quarter), bf16),
            vm((2, n_z, rows, eighth), bf16),
            vm((2, n_z, rows, eighth), bf16),
            vm((n_z - 1, rows, quarter), bf16),
            vm((n_z - 1, rows, quarter), bf16),
            vm((rows, quarter), f32),
            vm((more, rows, quarter), bf16),
            vm((more, rows, quarter), bf16),
            vm((QUAD, rows, quarter), bf16),
            dma((2, n_z - 1)), dma((2, n_z - 1)),
            dma((2, n_z - 1)), dma((2, n_z - 1)),
            dma((n_z,)), dma((n_z,)),
            dma((2, n_bits, CHUNKS)), dma((2, n_bits, CHUNKS)),
            dma((n_z,)), dma((n_z,)),
            dma((2, 2, n_z)), dma((2, 2, n_z)),
            dma((n_z - 1,)), dma((n_z - 1,)),
            dma((more,)), dma((more,)),
            dma((3,)), dma((3,)),
            vm((tokens, width), bf16), vm((tokens, width), bf16),
            vm((tokens, width), bf16), vm((tokens, width), bf16),
            vm(block_mask.shape[1:], jnp.int32), dma((6,)),
        ],
        compiler_params=pltpu.CompilerParams(
            collective_id=0, has_side_effects=True, vmem_limit_bytes=40 * 1024 * 1024
        ),
    )(*[pltpu.with_memory_space_constraint(a, pltpu.HBM) for a in (queries[0], keys[0], values[0], out_grad[0], out_weight, block_mask[0])])
    outs = pl.pallas_call(
        store,
        out_shape=[jax.ShapeDtypeStruct(o.shape, o.dtype) for o in outs],
        in_specs=[spec] * 5,
        out_specs=[pl.BlockSpec(memory_space=pltpu.HBM)] * 5,
        scratch_shapes=[dma((5,))],
        compiler_params=pltpu.CompilerParams(vmem_limit_bytes=4 * 1024 * 1024),
    )(*outs)
    return tuple(o[None] for o in outs[:4]) + (outs[4],)


def solution(mesh):
    token_spec = P("dp", "seq", None)
    row_spec = P("dp", None)
    return jax.shard_map(
        functools.partial(on_device, mesh.shape["seq"], mesh.shape["dp"]),
        mesh=mesh,
        in_specs=(token_spec,) * 4 + (row_spec, token_spec),
        out_specs=(token_spec,) * 4 + (row_spec,),
        check_vma=False,
    )
```

```python
import functools
import math

import jax
import jax.numpy as jnp
from jax import lax
from jax.experimental import pallas as pl
from jax.experimental.pallas import tpu as pltpu
from jax.sharding import PartitionSpec as P

H = 8
norm_eps = 1e-05
MESH = pl.DeviceIdType.MESH
f32 = jnp.float32
bf16 = jnp.bfloat16
QUAD = 4
CHUNKS = 4
UNROLL = 4


def bit(i, m):
    return lax.rem(lax.div(i, m), 2)


def flip(i, m):
    return i + m - 2 * m * bit(i, m)


def mm(a, b, da, db):
    return lax.dot_general(a, b, (((da,), (db,)), ((), ())), preferred_element_type=f32)


def over_heads(first, count, fn):
    def body(i, c):
        fn(first + i)
        return c

    lax.fori_loop(0, count, body, 0, unroll=min(UNROLL, count))


def visibility(mask, tokens):
    blocks = mask.shape[0]
    width = tokens // blocks
    t = lax.broadcasted_iota(jnp.int32, (tokens, blocks), 0)
    b = lax.broadcasted_iota(jnp.int32, (tokens, blocks), 1) * width
    member = jnp.where((t >= b) & (t < b + width), 1.0, 0.0)
    r = lax.broadcasted_iota(jnp.int32, (blocks, blocks), 0)
    c = lax.broadcasted_iota(jnp.int32, (blocks, blocks), 1)
    lower = jnp.where((mask == 1) & (c < r), 1.0, 0.0)
    member = member.astype(bf16)
    rows = mm(member, lower.astype(bf16), 1, 0).astype(bf16)
    earlier = mm(rows, member, 1, 1)
    same = mm(member, member, 1, 1)
    row = lax.broadcasted_iota(jnp.int32, (tokens, tokens), 0)
    col = lax.broadcasted_iota(jnp.int32, (tokens, tokens), 1)
    return earlier + jnp.where(col <= row, same, 0.0)


def kernel(
    n_seq, n_dp, q_hbm, k_hbm, v_hbm, g_hbm, w_ref, mask_hbm,
    out_ref, qg_ref, kg_ref, vg_ref, wg_ref,
    w_full, vis_ref, s_out, s_in, acc, prior, later, wts, attn, inv, normed,
    dnormed, dattn, dsc, term, a_in, u_out, *rest,
):
    first_in, mid_out, second_in, rest = rest[:2], rest[2:4], rest[4:6], rest[6:]
    z_out, z_in, z_own, c_in, c_own, c_got, r_out, r_in, f_all, *rest = rest
    w1_s, w1_r, w2_s, w2_r, w3_s, w3_r, st_s, st_r, a_s, a_r, x_s, x_r, z_s, z_r, *rest = rest
    c_s, c_r, t_s, t_r, r_s, r_r, f_s, f_r, q_ref, k_ref, v_ref, g_ref, mask_ref, in_s = rest
    tokens, width = q_ref.shape
    size = width // H
    n_z = n_dp // 2
    rows = w_ref.shape[0]
    cols = w_ref.shape[1]
    quarter = cols // QUAD
    eighth = quarter // 2
    hr = rows // 2
    scale = 1.0 / math.sqrt(n_seq * n_dp * tokens)
    n_bits = n_seq.bit_length() - 1
    s = lax.axis_index("seq")
    d = lax.axis_index("dp")
    z = lax.div(d, 2)
    core = lax.rem(d, 2)
    peer = flip(d, 1)
    seq_peer = {1: flip(s, 1), 2: flip(s, 2), 3: flip(flip(s, 1), 2)}
    bits = (bit(s, 1), bit(s, 2))
    zb = n_z // CHUNKS
    half = width // CHUNKS
    per = H // CHUNKS

    def qcols(seq_index):
        return pl.ds(pl.multiple_of(lax.rem(seq_index, QUAD) * quarter, quarter), quarter)

    def brow(dp_index):
        return pl.ds(pl.multiple_of(dp_index * rows, rows), rows)

    def hcols(h):
        return pl.ds(pl.multiple_of(h * size, size), size)

    def up(k):
        return lax.rem(z + k, n_z)

    def down(k):
        return lax.rem(z + n_z - k, n_z)

    def chunk_at(i):
        return lax.rem(lax.div(z, zb) + 1 + i, CHUNKS)

    def chunk(i):
        return pl.ds(pl.multiple_of(chunk_at(i) * half, half), half)

    def heads_of(i, fn):
        over_heads(chunk_at(i) * per, per, fn)

    def rc(src, dst, ss, rs, dev):
        return pltpu.make_async_remote_copy(
            src_ref=src, dst_ref=dst, send_sem=ss, recv_sem=rs, device_id=dev,
            device_id_type=MESH,
        )

    sent = []

    def go(*a, when=None):
        c = rc(*a)
        if when is None:
            c.start()
        else:
            pl.when(when)(c.start)
        sent.append((c, when))

    def arrive(dst, ss, rs, dev):
        rc(dst, dst, ss, rs, dev).wait_recv()

    loads = {}
    pairs = [(k_hbm, k_ref), (v_hbm, v_ref), (q_hbm, q_ref), (mask_hbm, mask_ref), (g_hbm, g_ref)]
    pairs.append((w_ref, w_full.at[brow(d)]))
    for i, name in enumerate("kvqmgw"):
        loads[name] = pltpu.make_async_copy(pairs[i][0], pairs[i][1], in_s.at[i])
        loads[name].start()

    barrier = pltpu.get_barrier_semaphore()
    partners = [(s, peer)]
    partners += [(seq_peer[j], d) for j in (1, 2, 3)]
    partners += [(flip(s, 1 << b), d) for b in range(2, n_bits)]
    partners += [(s, up(i) * 2 + core) for i in range(1, n_z)]
    for p in partners:
        pl.semaphore_signal(barrier, inc=1, device_id=p, device_id_type=MESH)
    acc[...] = jnp.zeros_like(acc)
    pl.semaphore_wait(barrier, len(partners))

    own_q = [qcols(s), qcols(seq_peer[3])]
    for qn in range(2):
        for i in range(1, n_z):
            go(
                w_ref.at[:, own_q[qn]], w_full.at[brow(d), own_q[qn]],
                w1_s.at[qn, i - 1], w1_r.at[qn, i - 1], (s, up(i) * 2 + core),
            )
    go(w_ref, w_full.at[brow(d)], w3_s.at[0], w3_r.at[0], (s, peer))
    loads["k"].wait()
    loads["v"].wait()

    def roles(way, b):
        own = bit(s, 1 << b)
        above = lax.div(s, 2 << b)
        last = (n_seq >> (b + 1)) - 1
        takes = own == 1 if way == 0 else own == 0
        if last == 0:
            return takes, None
        return takes, above != last if way == 0 else above != 0

    def send_state(way, b, i, when):
        go(
            s_out.at[way, b, chunk(i)], s_in.at[way, b, chunk(i)],
            st_s.at[way, b, i], st_r.at[way, b, i], (flip(s, 1 << b), d), when=when,
        )

    def first_state(way, i):
        takes, more = roles(way, 0)
        gives = jnp.logical_not(takes)
        send_state(way, 0, i, gives if more is None else jnp.logical_or(gives, more))

    def state_step(way, b, i):
        takes, more = roles(way, b)

        def receive():
            arrive(
                s_in.at[way, b, chunk(i)], st_s.at[way, b, i], st_r.at[way, b, i],
                (flip(s, 1 << b), d),
            )

        def pass_on():
            total = s_out[way, b, chunk(i)].astype(f32) + s_in[way, b, chunk(i)].astype(f32)
            s_out[way, b + 1, chunk(i)] = total.astype(bf16)

        def take():
            acc[chunk(i)] += s_in[way, b, chunk(i)].astype(f32)

        if more is None:
            pl.when(takes)(receive)
        else:
            pl.when(jnp.logical_or(takes, more))(receive)
            pl.when(more)(pass_on)
            send_state(way, b + 1, i, more)
        pl.when(takes)(take)

    def make_state(h):
        st = mm(k_ref[:, hcols(h)], v_ref[:, hcols(h)], 0, 0)
        s_out[0, 0, hcols(h)] = st.astype(bf16)

    for i in (0, 1, 2, 3):
        heads_of(i, make_state)
        first_state(0, i)

    loads["q"].wait()
    loads["m"].wait()
    vis_ref[...] = visibility(mask_ref[...], tokens)

    def local_attn(h):
        sc = mm(q_ref[:, hcols(h)], k_ref[:, hcols(h)], 1, 1)
        wt = (sc * vis_ref[...]).astype(bf16)
        wts[h] = wt
        attn[:, hcols(h)] = mm(wt, v_ref[:, hcols(h)], 1, 0)

    for i in (0, 1, 2, 3):
        heads_of(i, local_attn)

    for i in (0, 1, 2, 3):
        state_step(0, 0, i)

    for i in range(1, n_z):
        src = down(i) * 2 + core
        arrive(w_full.at[brow(src), own_q[0]], w1_s.at[0, i - 1], w1_r.at[0, i - 1], (s, src))
        for j in (1, 2):
            go(
                w_full.at[brow(src), own_q[0]], w_full.at[brow(src), own_q[0]],
                w2_s.at[j - 1, i - 1], w2_r.at[j - 1, i - 1], (seq_peer[j], d),
            )

    loads["g"].wait()
    loads["w"].wait()

    def finish_attn(h):
        a = attn[:, hcols(h)] + mm(q_ref[:, hcols(h)], prior[hcols(h), :], 1, 0)
        iv = lax.rsqrt(jnp.mean(a * a, -1, keepdims=True) + norm_eps)
        u = a * iv
        attn[:, hcols(h)] = u
        inv[h] = iv
        n = u.astype(bf16)
        normed[:, hcols(h)] = n
        term[hcols(h), :] = mm(n, g_ref[...], 0, 0).astype(bf16)

    starts = (0, quarter)
    wide = (eighth, quarter)
    offs = (0, eighth)
    tail = slice(3 * quarter, 4 * quarter)

    def axes(side, block):
        turn = lax.rem(block + side, 2) == 0
        first = jnp.where(turn, seq_peer[1], seq_peer[2]), jnp.where(turn, bits[0], bits[1])
        second = jnp.where(turn, seq_peer[2], seq_peer[1]), jnp.where(turn, bits[1], bits[0])
        return first, second

    def lanes(side, b):
        return pl.ds(pl.multiple_of(starts[side] + b * wide[side], eighth), wide[side])

    def part(b):
        return pl.ds(pl.multiple_of(b * hr, hr), hr)

    def swap_cores(i):
        zz = up(i + 1)
        go(term.at[brow(zz * 2 + 1 - core)], a_in.at[i], a_s.at[i], a_r.at[i], (s, peer))

    def first_cut(i):
        zz = up(i + 1)
        arrive(a_in.at[i], a_s.at[i], a_r.at[i], (s, peer))
        u_out[i] = (term[brow(zz * 2 + core), :].astype(f32) + a_in[i].astype(f32)).astype(bf16)
        for side in (1, 0):
            (dev, b), _ = axes(side, zz)
            go(
                u_out.at[i, :, lanes(side, 1 - b)], first_in[side].at[i],
                x_s.at[0, side, i], x_r.at[0, side, i], (dev, d),
            )
        if i < n_z - 1:
            go(u_out.at[i, :, tail], c_in.at[i], c_s.at[i], c_r.at[i], (s, zz * 2 + core))

    def second_cut(i):
        for side in (1, 0):
            (dev, b), (dev2, b2) = axes(side, up(i + 1))
            arrive(first_in[side].at[i], x_s.at[0, side, i], x_r.at[0, side, i], (dev, d))
            got = first_in[side][i, part(1 - b2), :].astype(f32)
            own = u_out[i, part(1 - b2), lanes(side, b)].astype(f32)
            mid_out[side][i] = (own + got).astype(bf16)
            go(
                mid_out[side].at[i], second_in[side].at[i],
                x_s.at[1, side, i], x_r.at[1, side, i], (dev2, d),
            )

    def z_step(i):
        zz = up(i + 1)
        for side in (1, 0):
            (_, b), (dev2, b2) = axes(side, zz)
            arrive(second_in[side].at[i], x_s.at[1, side, i], x_r.at[1, side, i], (dev2, d))
            total = u_out[i, part(b2), lanes(side, b)].astype(f32)
            total = total + first_in[side][i, part(b2), :].astype(f32)
            total = total + second_in[side][i].astype(f32)
            at = slice(offs[side], offs[side] + wide[side])
            if i < n_z - 1:
                z_out[i, :, at] = total.astype(bf16)
            else:
                z_own[:, at] = total
        if i < n_z - 1:
            go(z_out.at[i], z_in.at[i], z_s.at[i], z_r.at[i], (s, zz * 2 + core))

    halves = (slice(0, hr), slice(hr, 2 * hr))

    def tail_first():
        total = u_out[n_z - 1, :, tail].astype(f32)
        for i in range(n_z - 1):
            arrive(c_in.at[i], c_s.at[i], c_r.at[i], (s, down(i + 1) * 2 + core))
            total = total + c_in[i].astype(f32)
        c_own[0] = total.astype(bf16)
        for h in (0, 1):
            go(c_own.at[0, halves[h]], c_got.at[0, halves[h]], t_s.at[0, h], t_r.at[0, h], (seq_peer[1 + h], d))

    def tail_second():
        for h in (0, 1):
            arrive(c_got.at[0, halves[h]], t_s.at[0, h], t_r.at[0, h], (seq_peer[1 + h], d))
            total = c_own[0, halves[h]].astype(f32) + c_got[0, halves[h]].astype(f32)
            c_own[1, halves[h]] = total.astype(bf16)
            go(c_own.at[1, halves[h]], c_got.at[1, halves[h]], t_s.at[1, h], t_r.at[1, h], (seq_peer[2 - h], d))

    def tail_last():
        for h in (0, 1):
            arrive(c_got.at[1, halves[h]], t_s.at[1, h], t_r.at[1, h], (seq_peer[2 - h], d))
        total = c_own[1].astype(f32) + c_got[1].astype(f32)
        for b in range(2, n_bits):
            own = total.astype(bf16)
            c_own[b] = own
            dev = (flip(s, 1 << b), d)
            go(c_own.at[b], c_got.at[b], t_s.at[b, 0], t_r.at[b, 0], dev)
            arrive(c_got.at[b], t_s.at[b, 0], t_r.at[b, 0], dev)
            total = own.astype(f32) + c_got[b].astype(f32)
        wg_ref[:, tail] = total * scale

    def grad_norm(h):
        dn = mm(g_ref[...], w_full[hcols(h), :], 1, 1)
        u = attn[:, hcols(h)]
        da = (inv[h] * (dn - u * jnp.mean(dn * u, -1, keepdims=True))).astype(bf16)
        dattn[:, hcols(h)] = da
        s_out[1, 0, hcols(h)] = mm(q_ref[:, hcols(h)], da, 0, 0).astype(bf16)

    def parts(i):
        return range(i * n_z // CHUNKS, (i + 1) * n_z // CHUNKS)

    def offsets_of(i):
        if zb == 1:
            return [CHUNKS - 1 - i]
        return list(range(n_z)) if i == CHUNKS - 1 else []

    def rows_over(i):
        for k in offsets_of(i):
            if k == 0:
                continue
            src = down(k) * 2 + core
            arrive(w_full.at[brow(src), own_q[1]], w1_s.at[1, k - 1], w1_r.at[1, k - 1], (s, src))
            for j in (1, 2):
                arrive(
                    w_full.at[brow(src), qcols(seq_peer[j])], w2_s.at[j - 1, k - 1],
                    w2_r.at[j - 1, k - 1], (seq_peer[j], d),
                )
            go(w_full.at[brow(src)], w_full.at[brow(src)], w3_s.at[k], w3_r.at[k], (s, peer))

    def rows_here(i):
        for k in offsets_of(i):
            src = down(k) * 2 + 1 - core
            arrive(w_full.at[brow(src)], w3_s.at[k], w3_r.at[k], (s, peer))

    def cut_again(i):
        for j in parts(i):
            second_cut(j)

    def last_cut(i):
        for j in parts(i):
            z_step(j)

    def every(i, last):
        if zb == 1:
            return [i]
        return list(range(n_z)) if last else []

    def finish(i, last=False):
        for b in range(1, n_bits):
            state_step(0, b, i)
        prior[chunk(i)] = acc[chunk(i)].astype(bf16)
        acc[chunk(i)] = jnp.zeros((half, size), f32)
        heads_of(i, finish_attn)
        for j in every(i, last):
            swap_cores(j)

    def cut_first(i, last=False):
        for j in every(i, last):
            first_cut(j)

    finish(0)
    finish(1)
    cut_first(0)
    finish(2)
    cut_first(1)
    finish(3, True)
    cut_first(2)
    rows_over(2)
    rows_over(3)
    rows_here(3)
    heads_of(3, grad_norm)
    first_state(1, 3)
    cut_first(3, True)
    rows_over(1)
    cut_again(0)
    rows_here(2)
    heads_of(2, grad_norm)
    first_state(1, 2)
    rows_over(0)
    cut_again(1)
    rows_here(1)
    heads_of(1, grad_norm)
    first_state(1, 1)
    cut_again(2)
    rows_here(0)
    heads_of(0, grad_norm)
    first_state(1, 0)
    cut_again(3)

    def make_scores(h):
        ds = (mm(dattn[:, hcols(h)], v_ref[:, hcols(h)], 1, 1) * vis_ref[...]).astype(bf16)
        dsc[h] = ds
        qg = mm(ds, k_ref[:, hcols(h)], 1, 0) + mm(dattn[:, hcols(h)], prior[hcols(h), :], 1, 1)
        qg_ref[:, hcols(h)] = qg.astype(bf16)
        out_ref[:, hcols(h)] = mm(normed[...], w_full[:, hcols(h)], 1, 0).astype(bf16)

    heads_of(3, make_scores)
    last_cut(0)
    state_step(1, 0, 3)
    heads_of(2, make_scores)
    last_cut(1)
    tail_first()
    state_step(1, 0, 2)
    heads_of(1, make_scores)
    last_cut(2)
    state_step(1, 0, 1)
    heads_of(0, make_scores)
    last_cut(3)
    state_step(1, 0, 0)
    tail_second()

    def local_grads(h):
        attn[:, hcols(h)] = mm(dsc[h], q_ref[:, hcols(h)], 0, 0)
        dnormed[:, hcols(h)] = mm(wts[h], dattn[:, hcols(h)], 0, 0)

    for i in reversed(range(CHUNKS)):
        heads_of(i, local_grads)

    total = z_own[...]
    for i in range(n_z - 1):
        src = down(i + 1) * 2 + core
        arrive(z_in.at[i], z_s.at[i], z_r.at[i], (s, src))
        total = total + z_in[i].astype(f32)
    for b in range(2, n_bits):
        own = total.astype(bf16)
        r_out[b - 2] = own
        dev = (flip(s, 1 << b), d)
        go(r_out.at[b - 2], r_in.at[b - 2], r_s.at[b - 2], r_r.at[b - 2], dev)
        arrive(r_in.at[b - 2], r_s.at[b - 2], r_r.at[b - 2], dev)
        total = own.astype(f32) + r_in[b - 2].astype(f32)
    place = lax.rem(s, QUAD)
    f_all[place] = total.astype(bf16)
    for j in (1, 2, 3):
        go(f_all.at[place], f_all.at[place], f_s.at[j - 1], f_r.at[j - 1], (seq_peer[j], d))

    tail_last()

    def last_grads(h):
        kg = attn[:, hcols(h)] + mm(v_ref[:, hcols(h)], later[hcols(h), :], 1, 1)
        kg_ref[:, hcols(h)] = kg.astype(bf16)
        vg = dnormed[:, hcols(h)] + mm(k_ref[:, hcols(h)], later[hcols(h), :], 1, 0)
        vg_ref[:, hcols(h)] = vg.astype(bf16)

    for i in reversed(range(CHUNKS)):
        for b in range(1, n_bits):
            state_step(1, b, i)
        later[chunk(i)] = acc[chunk(i)].astype(bf16)
        heads_of(i, last_grads)

    for j in (1, 2, 3):
        there = lax.rem(seq_peer[j], QUAD)
        arrive(f_all.at[there], f_s.at[j - 1], f_r.at[j - 1], (seq_peer[j], d))
    for p in range(QUAD):
        for side in (0, 1):
            turn = lax.rem(z + side, 2) == 0
            b, b2 = jnp.where(turn, p % 2, p // 2), jnp.where(turn, p // 2, p % 2)
            got = f_all[p, :, offs[side]:offs[side] + wide[side]]
            wg_ref[part(b2), lanes(side, b)] = got.astype(f32) * scale
    for c, when in sent:
        if when is None:
            c.wait_send()
        else:
            pl.when(when)(c.wait_send)


def store(*refs):
    src, dst, sems = refs[:5], refs[5:10], refs[10]
    saves = [pltpu.make_async_copy(src[i], dst[i], sems.at[i]) for i in range(5)]
    for c in saves:
        c.start()
    for c in saves:
        c.wait()


def on_device(n_seq, n_dp, queries, keys, values, out_grad, out_weight, block_mask):
    _, tokens, width = queries.shape
    rows, cols = out_weight.shape
    size = width // H
    n_z = n_dp // 2
    n_bits = n_seq.bit_length() - 1
    more = max(n_bits - 2, 1)
    quarter = cols // QUAD
    eighth = quarter // 2
    kept = quarter + eighth
    half_rows = rows // 2
    dma = pltpu.SemaphoreType.DMA
    vm = pltpu.VMEM
    act = jax.ShapeDtypeStruct((tokens, width), bf16)
    spec = pl.BlockSpec(memory_space=pltpu.VMEM)
    outs = pl.pallas_call(
        functools.partial(kernel, n_seq, n_dp),
        out_shape=[vm((tokens, width), bf16)] * 4 + [vm((rows, cols), f32)],
        in_specs=[pl.BlockSpec(memory_space=pltpu.HBM)] * 6,
        out_specs=[spec] * 5,
        scratch_shapes=[
            vm((width, cols), bf16),
            vm((tokens, tokens), f32),
            vm((2, n_bits, width, size), bf16),
            vm((2, n_bits, width, size), bf16),
            vm((width, size), f32),
            vm((width, size), bf16),
            vm((width, size), bf16),
            vm((H, tokens, tokens), bf16),
            vm((tokens, width), f32),
            vm((H, tokens, 1), f32),
            vm((tokens, width), bf16),
            vm((tokens, width), f32),
            vm((tokens, width), bf16),
            vm((H, tokens, tokens), bf16),
            vm((width, cols), bf16),
            vm((n_z, rows, cols), bf16),
            vm((n_z, rows, cols), bf16),
            vm((n_z, rows, eighth), bf16), vm((n_z, rows, quarter), bf16),
            vm((n_z, half_rows, eighth), bf16), vm((n_z, half_rows, quarter), bf16),
            vm((n_z, half_rows, eighth), bf16), vm((n_z, half_rows, quarter), bf16),
            vm((n_z - 1, half_rows, kept), bf16),
            vm((n_z - 1, half_rows, kept), bf16),
            vm((half_rows, kept), f32),
            vm((n_z - 1, rows, quarter), bf16),
            vm((n_bits, rows, quarter), bf16),
            vm((n_bits, rows, quarter), bf16),
            vm((more, half_rows, kept), bf16),
            vm((more, half_rows, kept), bf16),
            vm((QUAD, half_rows, kept), bf16),
            dma((2, n_z - 1)), dma((2, n_z - 1)),
            dma((2, n_z - 1)), dma((2, n_z - 1)),
            dma((n_z,)), dma((n_z,)),
            dma((2, n_bits, CHUNKS)), dma((2, n_bits, CHUNKS)),
            dma((n_z,)), dma((n_z,)),
            dma((2, 2, n_z)), dma((2, 2, n_z)),
            dma((n_z - 1,)), dma((n_z - 1,)),
            dma((n_z - 1,)), dma((n_z - 1,)),
            dma((n_bits, 2)), dma((n_bits, 2)),
            dma((more,)), dma((more,)),
            dma((3,)), dma((3,)),
            vm((tokens, width), bf16), vm((tokens, width), bf16),
            vm((tokens, width), bf16), vm((tokens, width), bf16),
            vm(block_mask.shape[1:], jnp.int32), dma((6,)),
        ],
        compiler_params=pltpu.CompilerParams(
            collective_id=0, has_side_effects=True, vmem_limit_bytes=40 * 1024 * 1024
        ),
    )(*[pltpu.with_memory_space_constraint(a, pltpu.HBM) for a in (queries[0], keys[0], values[0], out_grad[0], out_weight, block_mask[0])])
    outs = pl.pallas_call(
        store,
        out_shape=[jax.ShapeDtypeStruct(o.shape, o.dtype) for o in outs],
        in_specs=[spec] * 5,
        out_specs=[pl.BlockSpec(memory_space=pltpu.HBM)] * 5,
        scratch_shapes=[dma((5,))],
        compiler_params=pltpu.CompilerParams(vmem_limit_bytes=4 * 1024 * 1024),
    )(*outs)
    return tuple(o[None] for o in outs[:4]) + (outs[4],)


def solution(mesh):
    token_spec = P("dp", "seq", None)
    row_spec = P("dp", None)
    return jax.shard_map(
        functools.partial(on_device, mesh.shape["seq"], mesh.shape["dp"]),
        mesh=mesh,
        in_specs=(token_spec,) * 4 + (row_spec, token_spec),
        out_specs=(token_spec,) * 4 + (row_spec,),
        check_vma=False,
    )
```

```python
import functools
import math

import jax
import jax.numpy as jnp
from jax import lax
from jax.experimental import pallas as pl
from jax.experimental.pallas import tpu as pltpu
from jax.sharding import PartitionSpec as P

H = 8
norm_eps = 1e-05
MESH = pl.DeviceIdType.MESH
f32 = jnp.float32
bf16 = jnp.bfloat16
QUAD = 4
CHUNKS = 4
UNROLL = 4


def bit(i, m):
    return lax.rem(lax.div(i, m), 2)


def flip(i, m):
    return i + m - 2 * m * bit(i, m)


def mm(a, b, da, db):
    return lax.dot_general(a, b, (((da,), (db,)), ((), ())), preferred_element_type=f32)


def over_heads(first, count, fn):
    def body(i, c):
        fn(first + i)
        return c

    lax.fori_loop(0, count, body, 0, unroll=min(UNROLL, count))


def visibility(mask, tokens):
    blocks = mask.shape[0]
    width = tokens // blocks
    t = lax.broadcasted_iota(jnp.int32, (tokens, blocks), 0)
    b = lax.broadcasted_iota(jnp.int32, (tokens, blocks), 1) * width
    member = jnp.where((t >= b) & (t < b + width), 1.0, 0.0)
    r = lax.broadcasted_iota(jnp.int32, (blocks, blocks), 0)
    c = lax.broadcasted_iota(jnp.int32, (blocks, blocks), 1)
    lower = jnp.where((mask == 1) & (c < r), 1.0, 0.0)
    member = member.astype(bf16)
    rows = mm(member, lower.astype(bf16), 1, 0).astype(bf16)
    earlier = mm(rows, member, 1, 1)
    same = mm(member, member, 1, 1)
    row = lax.broadcasted_iota(jnp.int32, (tokens, tokens), 0)
    col = lax.broadcasted_iota(jnp.int32, (tokens, tokens), 1)
    return earlier + jnp.where(col <= row, same, 0.0)


def kernel(
    n_seq, n_dp, q_hbm, k_hbm, v_hbm, g_hbm, w_ref, mask_hbm,
    out_ref, qg_ref, kg_ref, vg_ref, wg_ref,
    w_full, vis_ref, s_out, s_in, acc, prior, later, wts, attn, inv, normed,
    dnormed, dattn, dsc, term, a_in, u_out, *rest,
):
    first_in, mid_out, second_in, rest = rest[:2], rest[2:4], rest[4:6], rest[6:]
    z_out, z_in, z_own, c_in, c_own, c_got, r_out, r_in, f_all, *rest = rest
    w1_s, w1_r, w2_s, w2_r, w3_s, w3_r, st_s, st_r, a_s, a_r, x_s, x_r, z_s, z_r, *rest = rest
    c_s, c_r, t_s, t_r, r_s, r_r, f_s, f_r, q_ref, k_ref, v_ref, g_ref, mask_ref, in_s = rest
    tokens, width = q_ref.shape
    size = width // H
    n_z = n_dp // 2
    rows = w_ref.shape[0]
    cols = w_ref.shape[1]
    quarter = cols // QUAD
    eighth = quarter // 2
    hr = rows // 2
    scale = 1.0 / math.sqrt(n_seq * n_dp * tokens)
    n_bits = n_seq.bit_length() - 1
    s = lax.axis_index("seq")
    d = lax.axis_index("dp")
    z = lax.div(d, 2)
    core = lax.rem(d, 2)
    peer = flip(d, 1)
    seq_peer = {1: flip(s, 1), 2: flip(s, 2), 3: flip(flip(s, 1), 2)}
    bits = (bit(s, 1), bit(s, 2))
    zb = n_z // CHUNKS
    half = width // CHUNKS
    per = H // CHUNKS

    def qcols(seq_index):
        return pl.ds(pl.multiple_of(lax.rem(seq_index, QUAD) * quarter, quarter), quarter)

    def brow(dp_index):
        return pl.ds(pl.multiple_of(dp_index * rows, rows), rows)

    def hcols(h):
        return pl.ds(pl.multiple_of(h * size, size), size)

    def up(k):
        return lax.rem(z + k, n_z)

    def down(k):
        return lax.rem(z + n_z - k, n_z)

    def chunk_at(i):
        return lax.rem(lax.div(z, zb) + 1 + i, CHUNKS)

    def chunk(i):
        return pl.ds(pl.multiple_of(chunk_at(i) * half, half), half)

    def heads_of(i, fn):
        over_heads(chunk_at(i) * per, per, fn)

    def rc(src, dst, ss, rs, dev):
        return pltpu.make_async_remote_copy(
            src_ref=src, dst_ref=dst, send_sem=ss, recv_sem=rs, device_id=dev,
            device_id_type=MESH,
        )

    sent = []

    def go(*a, when=None):
        c = rc(*a)
        if when is None:
            c.start()
        else:
            pl.when(when)(c.start)
        sent.append((c, when))

    def arrive(dst, ss, rs, dev):
        rc(dst, dst, ss, rs, dev).wait_recv()

    loads = {}
    pairs = [(k_hbm, k_ref), (v_hbm, v_ref), (q_hbm, q_ref), (mask_hbm, mask_ref), (g_hbm, g_ref)]
    pairs.append((w_ref, w_full.at[brow(d)]))
    for i, name in enumerate("kvqmgw"):
        loads[name] = pltpu.make_async_copy(pairs[i][0], pairs[i][1], in_s.at[i])
        loads[name].start()

    barrier = pltpu.get_barrier_semaphore()
    partners = [(s, peer)]
    partners += [(seq_peer[j], d) for j in (1, 2, 3)]
    partners += [(flip(s, 1 << b), d) for b in range(2, n_bits)]
    partners += [(s, up(i) * 2 + core) for i in range(1, n_z)]
    for p in partners:
        pl.semaphore_signal(barrier, inc=1, device_id=p, device_id_type=MESH)
    acc[...] = jnp.zeros_like(acc)
    pl.semaphore_wait(barrier, len(partners))

    own_q = [qcols(s), qcols(seq_peer[3])]
    for qn in range(2):
        for i in range(1, n_z):
            go(
                w_ref.at[:, own_q[qn]], w_full.at[brow(d), own_q[qn]],
                w1_s.at[qn, i - 1], w1_r.at[qn, i - 1], (s, up(i) * 2 + core),
            )
    go(w_ref, w_full.at[brow(d)], w3_s.at[0], w3_r.at[0], (s, peer))
    loads["k"].wait()
    loads["v"].wait()

    def roles(way, b):
        own = bit(s, 1 << b)
        above = lax.div(s, 2 << b)
        last = (n_seq >> (b + 1)) - 1
        takes = own == 1 if way == 0 else own == 0
        if last == 0:
            return takes, None
        return takes, above != last if way == 0 else above != 0

    def head_rows(i, k):
        return hcols(chunk_at(i) * per + k)

    def send_state(way, b, i, k, when):
        go(
            s_out.at[way, b, head_rows(i, k)], s_in.at[way, b, head_rows(i, k)],
            st_s.at[way, b, i * per + k], st_r.at[way, b, i * per + k], (flip(s, 1 << b), d),
            when=when,
        )

    def first_state(way, i, fn):
        takes, more = roles(way, 0)
        gives = jnp.logical_not(takes)
        for k in range(per):
            over_heads(chunk_at(i) * per + k, 1, fn)
            send_state(way, 0, i, k, gives if more is None else jnp.logical_or(gives, more))

    def state_step(way, b, i):
        for k in range(per):
            head_step(way, b, i, k)

    def head_step(way, b, i, k):
        takes, more = roles(way, b)
        at = head_rows(i, k)

        def receive():
            arrive(
                s_in.at[way, b, at], st_s.at[way, b, i * per + k], st_r.at[way, b, i * per + k],
                (flip(s, 1 << b), d),
            )

        def pass_on():
            total = s_out[way, b, at].astype(f32) + s_in[way, b, at].astype(f32)
            s_out[way, b + 1, at] = total.astype(bf16)

        def take():
            acc[at] += s_in[way, b, at].astype(f32)

        if more is None:
            pl.when(takes)(receive)
        else:
            pl.when(jnp.logical_or(takes, more))(receive)
            pl.when(more)(pass_on)
            send_state(way, b + 1, i, k, more)
        pl.when(takes)(take)

    def make_state(h):
        st = mm(k_ref[:, hcols(h)], v_ref[:, hcols(h)], 0, 0)
        s_out[0, 0, hcols(h)] = st.astype(bf16)

    for i in (0, 1, 2, 3):
        first_state(0, i, make_state)

    loads["q"].wait()
    loads["m"].wait()
    vis_ref[...] = visibility(mask_ref[...], tokens)

    def local_attn(h):
        sc = mm(q_ref[:, hcols(h)], k_ref[:, hcols(h)], 1, 1)
        wt = (sc * vis_ref[...]).astype(bf16)
        wts[h] = wt
        attn[:, hcols(h)] = mm(wt, v_ref[:, hcols(h)], 1, 0)

    for i in (0, 1, 2, 3):
        heads_of(i, local_attn)

    for i in (0, 1, 2, 3):
        state_step(0, 0, i)

    for i in range(1, n_z):
        src = down(i) * 2 + core
        arrive(w_full.at[brow(src), own_q[0]], w1_s.at[0, i - 1], w1_r.at[0, i - 1], (s, src))
        for j in (1, 2):
            go(
                w_full.at[brow(src), own_q[0]], w_full.at[brow(src), own_q[0]],
                w2_s.at[j - 1, i - 1], w2_r.at[j - 1, i - 1], (seq_peer[j], d),
            )

    loads["g"].wait()
    loads["w"].wait()

    def finish_attn(h):
        a = attn[:, hcols(h)] + mm(q_ref[:, hcols(h)], prior[hcols(h), :], 1, 0)
        iv = lax.rsqrt(jnp.mean(a * a, -1, keepdims=True) + norm_eps)
        u = a * iv
        attn[:, hcols(h)] = u
        inv[h] = iv
        n = u.astype(bf16)
        normed[:, hcols(h)] = n
        term[hcols(h), :] = mm(n, g_ref[...], 0, 0).astype(bf16)

    starts = (0, quarter)
    wide = (eighth, quarter)
    offs = (0, eighth)
    tail = slice(3 * quarter, 4 * quarter)

    def axes(side, block):
        turn = lax.rem(block + side, 2) == 0
        first = jnp.where(turn, seq_peer[1], seq_peer[2]), jnp.where(turn, bits[0], bits[1])
        second = jnp.where(turn, seq_peer[2], seq_peer[1]), jnp.where(turn, bits[1], bits[0])
        return first, second

    def lanes(side, b):
        return pl.ds(pl.multiple_of(starts[side] + b * wide[side], eighth), wide[side])

    def part(b):
        return pl.ds(pl.multiple_of(b * hr, hr), hr)

    def swap_cores(i):
        zz = up(i + 1)
        go(term.at[brow(zz * 2 + 1 - core)], a_in.at[i], a_s.at[i], a_r.at[i], (s, peer))

    def first_cut(i):
        zz = up(i + 1)
        arrive(a_in.at[i], a_s.at[i], a_r.at[i], (s, peer))
        u_out[i] = (term[brow(zz * 2 + core), :].astype(f32) + a_in[i].astype(f32)).astype(bf16)
        for side in (1, 0):
            (dev, b), _ = axes(side, zz)
            go(
                u_out.at[i, :, lanes(side, 1 - b)], first_in[side].at[i],
                x_s.at[0, side, i], x_r.at[0, side, i], (dev, d),
            )
        if i < n_z - 1:
            go(u_out.at[i, :, tail], c_in.at[i], c_s.at[i], c_r.at[i], (s, zz * 2 + core))

    def second_cut(i):
        for side in (1, 0):
            (dev, b), (dev2, b2) = axes(side, up(i + 1))
            arrive(first_in[side].at[i], x_s.at[0, side, i], x_r.at[0, side, i], (dev, d))
            got = first_in[side][i, part(1 - b2), :].astype(f32)
            own = u_out[i, part(1 - b2), lanes(side, b)].astype(f32)
            mid_out[side][i] = (own + got).astype(bf16)
            go(
                mid_out[side].at[i], second_in[side].at[i],
                x_s.at[1, side, i], x_r.at[1, side, i], (dev2, d),
            )

    def z_step(i):
        zz = up(i + 1)
        for side in (1, 0):
            (_, b), (dev2, b2) = axes(side, zz)
            arrive(second_in[side].at[i], x_s.at[1, side, i], x_r.at[1, side, i], (dev2, d))
            total = u_out[i, part(b2), lanes(side, b)].astype(f32)
            total = total + first_in[side][i, part(b2), :].astype(f32)
            total = total + second_in[side][i].astype(f32)
            at = slice(offs[side], offs[side] + wide[side])
            if i < n_z - 1:
                z_out[i, :, at] = total.astype(bf16)
            else:
                z_own[:, at] = total
        if i < n_z - 1:
            go(z_out.at[i], z_in.at[i], z_s.at[i], z_r.at[i], (s, zz * 2 + core))

    halves = (slice(0, hr), slice(hr, 2 * hr))

    def tail_first():
        total = u_out[n_z - 1, :, tail].astype(f32)
        for i in range(n_z - 1):
            arrive(c_in.at[i], c_s.at[i], c_r.at[i], (s, down(i + 1) * 2 + core))
            total = total + c_in[i].astype(f32)
        c_own[0] = total.astype(bf16)
        for h in (0, 1):
            go(c_own.at[0, halves[h]], c_got.at[0, halves[h]], t_s.at[0, h], t_r.at[0, h], (seq_peer[1 + h], d))

    def tail_second():
        for h in (0, 1):
            arrive(c_got.at[0, halves[h]], t_s.at[0, h], t_r.at[0, h], (seq_peer[1 + h], d))
            total = c_own[0, halves[h]].astype(f32) + c_got[0, halves[h]].astype(f32)
            c_own[1, halves[h]] = total.astype(bf16)
            go(c_own.at[1, halves[h]], c_got.at[1, halves[h]], t_s.at[1, h], t_r.at[1, h], (seq_peer[2 - h], d))

    def tail_last():
        for h in (0, 1):
            arrive(c_got.at[1, halves[h]], t_s.at[1, h], t_r.at[1, h], (seq_peer[2 - h], d))
        total = c_own[1].astype(f32) + c_got[1].astype(f32)
        for b in range(2, n_bits):
            own = total.astype(bf16)
            c_own[b] = own
            dev = (flip(s, 1 << b), d)
            go(c_own.at[b], c_got.at[b], t_s.at[b, 0], t_r.at[b, 0], dev)
            arrive(c_got.at[b], t_s.at[b, 0], t_r.at[b, 0], dev)
            total = own.astype(f32) + c_got[b].astype(f32)
        wg_ref[:, tail] = total * scale

    def grad_norm(h):
        dn = mm(g_ref[...], w_full[hcols(h), :], 1, 1)
        u = attn[:, hcols(h)]
        da = (inv[h] * (dn - u * jnp.mean(dn * u, -1, keepdims=True))).astype(bf16)
        dattn[:, hcols(h)] = da
        s_out[1, 0, hcols(h)] = mm(q_ref[:, hcols(h)], da, 0, 0).astype(bf16)

    def parts(i):
        return range(i * n_z // CHUNKS, (i + 1) * n_z // CHUNKS)

    def offsets_of(i):
        if zb == 1:
            return [CHUNKS - 1 - i]
        return list(range(n_z)) if i == CHUNKS - 1 else []

    def rows_over(i):
        for k in offsets_of(i):
            if k == 0:
                continue
            src = down(k) * 2 + core
            arrive(w_full.at[brow(src), own_q[1]], w1_s.at[1, k - 1], w1_r.at[1, k - 1], (s, src))
            for j in (1, 2):
                arrive(
                    w_full.at[brow(src), qcols(seq_peer[j])], w2_s.at[j - 1, k - 1],
                    w2_r.at[j - 1, k - 1], (seq_peer[j], d),
                )
            go(w_full.at[brow(src)], w_full.at[brow(src)], w3_s.at[k], w3_r.at[k], (s, peer))

    def rows_here(i):
        for k in offsets_of(i):
            src = down(k) * 2 + 1 - core
            arrive(w_full.at[brow(src)], w3_s.at[k], w3_r.at[k], (s, peer))

    def cut_again(i):
        for j in parts(i):
            second_cut(j)

    def last_cut(i):
        for j in parts(i):
            z_step(j)

    def every(i, last):
        if zb == 1:
            return [i]
        return list(range(n_z)) if last else []

    def finish(i, last=False):
        for b in range(1, n_bits):
            state_step(0, b, i)
        prior[chunk(i)] = acc[chunk(i)].astype(bf16)
        acc[chunk(i)] = jnp.zeros((half, size), f32)
        heads_of(i, finish_attn)
        for j in every(i, last):
            swap_cores(j)

    def cut_first(i, last=False):
        for j in every(i, last):
            first_cut(j)

    finish(0)
    finish(1)
    cut_first(0)
    finish(2)
    cut_first(1)
    finish(3, True)
    cut_first(2)
    rows_over(2)
    rows_over(3)
    rows_here(3)
    first_state(1, 3, grad_norm)
    cut_first(3, True)
    rows_over(1)
    cut_again(0)
    rows_here(2)
    first_state(1, 2, grad_norm)
    rows_over(0)
    cut_again(1)
    rows_here(1)
    first_state(1, 1, grad_norm)
    cut_again(2)
    rows_here(0)
    first_state(1, 0, grad_norm)
    cut_again(3)

    def make_scores(h):
        ds = (mm(dattn[:, hcols(h)], v_ref[:, hcols(h)], 1, 1) * vis_ref[...]).astype(bf16)
        dsc[h] = ds
        qg = mm(ds, k_ref[:, hcols(h)], 1, 0) + mm(dattn[:, hcols(h)], prior[hcols(h), :], 1, 1)
        qg_ref[:, hcols(h)] = qg.astype(bf16)
        out_ref[:, hcols(h)] = mm(normed[...], w_full[:, hcols(h)], 1, 0).astype(bf16)

    heads_of(3, make_scores)
    last_cut(0)
    state_step(1, 0, 3)
    heads_of(2, make_scores)
    last_cut(1)
    tail_first()
    state_step(1, 0, 2)
    heads_of(1, make_scores)
    last_cut(2)
    state_step(1, 0, 1)
    heads_of(0, make_scores)
    tail_second()
    last_cut(3)
    state_step(1, 0, 0)

    def local_grads(h):
        attn[:, hcols(h)] = mm(dsc[h], q_ref[:, hcols(h)], 0, 0)
        dnormed[:, hcols(h)] = mm(wts[h], dattn[:, hcols(h)], 0, 0)

    for i in reversed(range(CHUNKS)):
        heads_of(i, local_grads)

    total = z_own[...]
    for i in range(n_z - 1):
        src = down(i + 1) * 2 + core
        arrive(z_in.at[i], z_s.at[i], z_r.at[i], (s, src))
        total = total + z_in[i].astype(f32)
    for b in range(2, n_bits):
        own = total.astype(bf16)
        r_out[b - 2] = own
        dev = (flip(s, 1 << b), d)
        go(r_out.at[b - 2], r_in.at[b - 2], r_s.at[b - 2], r_r.at[b - 2], dev)
        arrive(r_in.at[b - 2], r_s.at[b - 2], r_r.at[b - 2], dev)
        total = own.astype(f32) + r_in[b - 2].astype(f32)
    place = lax.rem(s, QUAD)
    f_all[place] = total.astype(bf16)
    for j in (3, 1, 2):
        go(f_all.at[place], f_all.at[place], f_s.at[j - 1], f_r.at[j - 1], (seq_peer[j], d))

    tail_last()

    def last_grads(h):
        kg = attn[:, hcols(h)] + mm(v_ref[:, hcols(h)], later[hcols(h), :], 1, 1)
        kg_ref[:, hcols(h)] = kg.astype(bf16)
        vg = dnormed[:, hcols(h)] + mm(k_ref[:, hcols(h)], later[hcols(h), :], 1, 0)
        vg_ref[:, hcols(h)] = vg.astype(bf16)

    for i in reversed(range(CHUNKS)):
        for b in range(1, n_bits):
            state_step(1, b, i)
        later[chunk(i)] = acc[chunk(i)].astype(bf16)
        heads_of(i, last_grads)

    for j in (1, 2, 3):
        there = lax.rem(seq_peer[j], QUAD)
        arrive(f_all.at[there], f_s.at[j - 1], f_r.at[j - 1], (seq_peer[j], d))
    for p in range(QUAD):
        for side in (0, 1):
            turn = lax.rem(z + side, 2) == 0
            b, b2 = jnp.where(turn, p % 2, p // 2), jnp.where(turn, p // 2, p % 2)
            got = f_all[p, :, offs[side]:offs[side] + wide[side]]
            wg_ref[part(b2), lanes(side, b)] = got.astype(f32) * scale
    for c, when in sent:
        if when is None:
            c.wait_send()
        else:
            pl.when(when)(c.wait_send)


def store(*refs):
    src, dst, sems = refs[:5], refs[5:10], refs[10]
    saves = [pltpu.make_async_copy(src[i], dst[i], sems.at[i]) for i in range(5)]
    for c in saves:
        c.start()
    for c in saves:
        c.wait()


def on_device(n_seq, n_dp, queries, keys, values, out_grad, out_weight, block_mask):
    _, tokens, width = queries.shape
    rows, cols = out_weight.shape
    size = width // H
    n_z = n_dp // 2
    n_bits = n_seq.bit_length() - 1
    more = max(n_bits - 2, 1)
    quarter = cols // QUAD
    eighth = quarter // 2
    kept = quarter + eighth
    half_rows = rows // 2
    dma = pltpu.SemaphoreType.DMA
    vm = pltpu.VMEM
    act = jax.ShapeDtypeStruct((tokens, width), bf16)
    spec = pl.BlockSpec(memory_space=pltpu.VMEM)
    outs = pl.pallas_call(
        functools.partial(kernel, n_seq, n_dp),
        out_shape=[vm((tokens, width), bf16)] * 4 + [vm((rows, cols), f32)],
        in_specs=[pl.BlockSpec(memory_space=pltpu.HBM)] * 6,
        out_specs=[spec] * 5,
        scratch_shapes=[
            vm((width, cols), bf16),
            vm((tokens, tokens), f32),
            vm((2, n_bits, width, size), bf16),
            vm((2, n_bits, width, size), bf16),
            vm((width, size), f32),
            vm((width, size), bf16),
            vm((width, size), bf16),
            vm((H, tokens, tokens), bf16),
            vm((tokens, width), f32),
            vm((H, tokens, 1), f32),
            vm((tokens, width), bf16),
            vm((tokens, width), f32),
            vm((tokens, width), bf16),
            vm((H, tokens, tokens), bf16),
            vm((width, cols), bf16),
            vm((n_z, rows, cols), bf16),
            vm((n_z, rows, cols), bf16),
            vm((n_z, rows, eighth), bf16), vm((n_z, rows, quarter), bf16),
            vm((n_z, half_rows, eighth), bf16), vm((n_z, half_rows, quarter), bf16),
            vm((n_z, half_rows, eighth), bf16), vm((n_z, half_rows, quarter), bf16),
            vm((n_z - 1, half_rows, kept), bf16),
            vm((n_z - 1, half_rows, kept), bf16),
            vm((half_rows, kept), f32),
            vm((n_z - 1, rows, quarter), bf16),
            vm((n_bits, rows, quarter), bf16),
            vm((n_bits, rows, quarter), bf16),
            vm((more, half_rows, kept), bf16),
            vm((more, half_rows, kept), bf16),
            vm((QUAD, half_rows, kept), bf16),
            dma((2, n_z - 1)), dma((2, n_z - 1)),
            dma((2, n_z - 1)), dma((2, n_z - 1)),
            dma((n_z,)), dma((n_z,)),
            dma((2, n_bits, H)), dma((2, n_bits, H)),
            dma((n_z,)), dma((n_z,)),
            dma((2, 2, n_z)), dma((2, 2, n_z)),
            dma((n_z - 1,)), dma((n_z - 1,)),
            dma((n_z - 1,)), dma((n_z - 1,)),
            dma((n_bits, 2)), dma((n_bits, 2)),
            dma((more,)), dma((more,)),
            dma((3,)), dma((3,)),
            vm((tokens, width), bf16), vm((tokens, width), bf16),
            vm((tokens, width), bf16), vm((tokens, width), bf16),
            vm(block_mask.shape[1:], jnp.int32), dma((6,)),
        ],
        compiler_params=pltpu.CompilerParams(
            collective_id=0, has_side_effects=True, vmem_limit_bytes=40 * 1024 * 1024
        ),
    )(*[pltpu.with_memory_space_constraint(a, pltpu.HBM) for a in (queries[0], keys[0], values[0], out_grad[0], out_weight, block_mask[0])])
    outs = pl.pallas_call(
        store,
        out_shape=[jax.ShapeDtypeStruct(o.shape, o.dtype) for o in outs],
        in_specs=[spec] * 5,
        out_specs=[pl.BlockSpec(memory_space=pltpu.HBM)] * 5,
        scratch_shapes=[dma((5,))],
        compiler_params=pltpu.CompilerParams(vmem_limit_bytes=4 * 1024 * 1024),
    )(*outs)
    return tuple(o[None] for o in outs[:4]) + (outs[4],)


def solution(mesh):
    token_spec = P("dp", "seq", None)
    row_spec = P("dp", None)
    return jax.shard_map(
        functools.partial(on_device, mesh.shape["seq"], mesh.shape["dp"]),
        mesh=mesh,
        in_specs=(token_spec,) * 4 + (row_spec, token_spec),
        out_specs=(token_spec,) * 4 + (row_spec,),
        check_vma=False,
    )
```

```python
import functools
import math

import jax
import jax.numpy as jnp
from jax import lax
from jax.experimental import pallas as pl
from jax.experimental.pallas import tpu as pltpu
from jax.sharding import PartitionSpec as P

H = 8
norm_eps = 1e-05
MESH = pl.DeviceIdType.MESH
f32 = jnp.float32
bf16 = jnp.bfloat16
QUAD = 4
CHUNKS = 4
UNROLL = 4


def bit(i, m):
    return lax.rem(lax.div(i, m), 2)


def flip(i, m):
    return i + m - 2 * m * bit(i, m)


def mm(a, b, da, db):
    return lax.dot_general(a, b, (((da,), (db,)), ((), ())), preferred_element_type=f32)


def over_heads(first, count, fn):
    def body(i, c):
        fn(first + i)
        return c

    lax.fori_loop(0, count, body, 0, unroll=min(UNROLL, count))


def visibility(mask, tokens):
    blocks = mask.shape[0]
    width = tokens // blocks
    t = lax.broadcasted_iota(jnp.int32, (tokens, blocks), 0)
    b = lax.broadcasted_iota(jnp.int32, (tokens, blocks), 1) * width
    member = jnp.where((t >= b) & (t < b + width), 1.0, 0.0)
    r = lax.broadcasted_iota(jnp.int32, (blocks, blocks), 0)
    c = lax.broadcasted_iota(jnp.int32, (blocks, blocks), 1)
    lower = jnp.where((mask == 1) & (c < r), 1.0, 0.0)
    member = member.astype(bf16)
    rows = mm(member, lower.astype(bf16), 1, 0).astype(bf16)
    earlier = mm(rows, member, 1, 1)
    same = mm(member, member, 1, 1)
    row = lax.broadcasted_iota(jnp.int32, (tokens, tokens), 0)
    col = lax.broadcasted_iota(jnp.int32, (tokens, tokens), 1)
    return earlier + jnp.where(col <= row, same, 0.0)


def kernel(
    n_seq, n_dp, q_hbm, k_hbm, v_hbm, g_hbm, w_ref, mask_hbm,
    out_ref, qg_ref, kg_ref, vg_ref, wg_ref,
    w_full, vis_ref, s_out, s_in, acc, prior, later, wts, attn, inv, normed,
    dnormed, dattn, dsc, term, a_in, u_out, *rest,
):
    first_in, mid_out, second_in, rest = rest[:2], rest[2:4], rest[4:6], rest[6:]
    z_out, z_in, z_own, c_in, c_own, c_got, r_out, r_in, f_all, *rest = rest
    w1_s, w1_r, w2_s, w2_r, w3_s, w3_r, st_s, st_r, a_s, a_r, x_s, x_r, z_s, z_r, *rest = rest
    c_s, c_r, t_s, t_r, r_s, r_r, f_s, f_r, q_ref, k_ref, v_ref, g_ref, mask_ref, in_s = rest
    tokens, width = q_ref.shape
    size = width // H
    n_z = n_dp // 2
    rows = w_ref.shape[0]
    cols = w_ref.shape[1]
    quarter = cols // QUAD
    eighth = quarter // 2
    hr = rows // 2
    scale = 1.0 / math.sqrt(n_seq * n_dp * tokens)
    n_bits = n_seq.bit_length() - 1
    s = lax.axis_index("seq")
    d = lax.axis_index("dp")
    z = lax.div(d, 2)
    core = lax.rem(d, 2)
    peer = flip(d, 1)
    seq_peer = {1: flip(s, 1), 2: flip(s, 2), 3: flip(flip(s, 1), 2)}
    bits = (bit(s, 1), bit(s, 2))
    zb = n_z // CHUNKS
    half = width // CHUNKS
    per = H // CHUNKS

    def qcols(seq_index):
        return pl.ds(pl.multiple_of(lax.rem(seq_index, QUAD) * quarter, quarter), quarter)

    def brow(dp_index):
        return pl.ds(pl.multiple_of(dp_index * rows, rows), rows)

    def hcols(h):
        return pl.ds(pl.multiple_of(h * size, size), size)

    def up(k):
        return lax.rem(z + k, n_z)

    def down(k):
        return lax.rem(z + n_z - k, n_z)

    def chunk_at(i):
        return lax.rem(lax.div(z, zb) + 1 + i, CHUNKS)

    def chunk(i):
        return pl.ds(pl.multiple_of(chunk_at(i) * half, half), half)

    def heads_of(i, fn):
        over_heads(chunk_at(i) * per, per, fn)

    def rc(src, dst, ss, rs, dev):
        return pltpu.make_async_remote_copy(
            src_ref=src, dst_ref=dst, send_sem=ss, recv_sem=rs, device_id=dev,
            device_id_type=MESH,
        )

    sent = []

    def go(*a, when=None):
        c = rc(*a)
        if when is None:
            c.start()
        else:
            pl.when(when)(c.start)
        sent.append((c, when))

    def arrive(dst, ss, rs, dev):
        rc(dst, dst, ss, rs, dev).wait_recv()

    loads = {}
    pairs = [(k_hbm, k_ref), (v_hbm, v_ref), (q_hbm, q_ref), (mask_hbm, mask_ref), (g_hbm, g_ref)]
    pairs.append((w_ref, w_full.at[brow(d)]))
    for i, name in enumerate("kvqmgw"):
        loads[name] = pltpu.make_async_copy(pairs[i][0], pairs[i][1], in_s.at[i])
        loads[name].start()

    barrier = pltpu.get_barrier_semaphore()
    partners = [(s, peer)]
    partners += [(seq_peer[j], d) for j in (1, 2, 3)]
    partners += [(flip(s, 1 << b), d) for b in range(2, n_bits)]
    partners += [(s, up(i) * 2 + core) for i in range(1, n_z)]
    for p in partners:
        pl.semaphore_signal(barrier, inc=1, device_id=p, device_id_type=MESH)
    acc[...] = jnp.zeros_like(acc)
    pl.semaphore_wait(barrier, len(partners))

    own_q = [qcols(s), qcols(seq_peer[3])]
    for qn in range(2):
        for i in range(1, n_z):
            go(
                w_ref.at[:, own_q[qn]], w_full.at[brow(d), own_q[qn]],
                w1_s.at[qn, i - 1], w1_r.at[qn, i - 1], (s, up(i) * 2 + core),
            )
    go(w_ref, w_full.at[brow(d)], w3_s.at[0], w3_r.at[0], (s, peer))
    loads["k"].wait()
    loads["v"].wait()

    def roles(way, b):
        own = bit(s, 1 << b)
        above = lax.div(s, 2 << b)
        last = (n_seq >> (b + 1)) - 1
        takes = own == 1 if way == 0 else own == 0
        if last == 0:
            return takes, None
        return takes, above != last if way == 0 else above != 0

    def head_rows(i, k):
        return hcols(chunk_at(i) * per + k)

    def send_state(way, b, i, k, when):
        go(
            s_out.at[way, b, head_rows(i, k)], s_in.at[way, b, head_rows(i, k)],
            st_s.at[way, b, i * per + k], st_r.at[way, b, i * per + k], (flip(s, 1 << b), d),
            when=when,
        )

    def first_state(way, i, fn):
        takes, more = roles(way, 0)
        gives = jnp.logical_not(takes)
        for k in range(per):
            over_heads(chunk_at(i) * per + k, 1, fn)
            send_state(way, 0, i, k, gives if more is None else jnp.logical_or(gives, more))

    def state_step(way, b, i):
        for k in range(per):
            head_step(way, b, i, k)

    def head_step(way, b, i, k):
        takes, more = roles(way, b)
        at = head_rows(i, k)

        def receive():
            arrive(
                s_in.at[way, b, at], st_s.at[way, b, i * per + k], st_r.at[way, b, i * per + k],
                (flip(s, 1 << b), d),
            )

        def pass_on():
            total = s_out[way, b, at].astype(f32) + s_in[way, b, at].astype(f32)
            s_out[way, b + 1, at] = total.astype(bf16)

        def take():
            acc[at] += s_in[way, b, at].astype(f32)

        if more is None:
            pl.when(takes)(receive)
        else:
            pl.when(jnp.logical_or(takes, more))(receive)
            pl.when(more)(pass_on)
            send_state(way, b + 1, i, k, more)
        pl.when(takes)(take)

    def make_state(h):
        st = mm(k_ref[:, hcols(h)], v_ref[:, hcols(h)], 0, 0)
        s_out[0, 0, hcols(h)] = st.astype(bf16)

    for i in (0, 1, 2, 3):
        first_state(0, i, make_state)

    loads["q"].wait()
    loads["m"].wait()
    vis_ref[...] = visibility(mask_ref[...], tokens)

    def local_attn(h):
        sc = mm(q_ref[:, hcols(h)], k_ref[:, hcols(h)], 1, 1)
        wt = (sc * vis_ref[...]).astype(bf16)
        wts[h] = wt
        attn[:, hcols(h)] = mm(wt, v_ref[:, hcols(h)], 1, 0)

    for i in (0, 1, 2, 3):
        heads_of(i, local_attn)

    for i in (0, 1, 2, 3):
        state_step(0, 0, i)

    for i in range(1, n_z):
        src = down(i) * 2 + core
        arrive(w_full.at[brow(src), own_q[0]], w1_s.at[0, i - 1], w1_r.at[0, i - 1], (s, src))
        for j in (1, 2):
            go(
                w_full.at[brow(src), own_q[0]], w_full.at[brow(src), own_q[0]],
                w2_s.at[j - 1, i - 1], w2_r.at[j - 1, i - 1], (seq_peer[j], d),
            )

    loads["g"].wait()
    loads["w"].wait()

    def finish_attn(h):
        a = attn[:, hcols(h)] + mm(q_ref[:, hcols(h)], prior[hcols(h), :], 1, 0)
        iv = lax.rsqrt(jnp.mean(a * a, -1, keepdims=True) + norm_eps)
        u = a * iv
        attn[:, hcols(h)] = u
        inv[h] = iv
        n = u.astype(bf16)
        normed[:, hcols(h)] = n
        term[hcols(h), :] = mm(n, g_ref[...], 0, 0).astype(bf16)

    starts = (0, quarter)
    wide = (eighth, quarter)
    offs = (0, eighth)
    tail = slice(3 * quarter, 4 * quarter)

    def axes(side, block):
        turn = lax.rem(block + side, 2) == 0
        first = jnp.where(turn, seq_peer[1], seq_peer[2]), jnp.where(turn, bits[0], bits[1])
        second = jnp.where(turn, seq_peer[2], seq_peer[1]), jnp.where(turn, bits[1], bits[0])
        return first, second

    def lanes(side, b):
        return pl.ds(pl.multiple_of(starts[side] + b * wide[side], eighth), wide[side])

    def part(b):
        return pl.ds(pl.multiple_of(b * hr, hr), hr)

    def swap_cores(i):
        zz = up(i + 1)
        go(term.at[brow(zz * 2 + 1 - core)], a_in.at[i], a_s.at[i], a_r.at[i], (s, peer))

    def first_cut(i):
        zz = up(i + 1)
        arrive(a_in.at[i], a_s.at[i], a_r.at[i], (s, peer))
        u_out[i] = (term[brow(zz * 2 + core), :].astype(f32) + a_in[i].astype(f32)).astype(bf16)
        for side in (1, 0):
            (dev, b), _ = axes(side, zz)
            go(
                u_out.at[i, :, lanes(side, 1 - b)], first_in[side].at[i],
                x_s.at[0, side, i], x_r.at[0, side, i], (dev, d),
            )
        if i < n_z - 1:
            go(u_out.at[i, :, tail], c_in.at[i], c_s.at[i], c_r.at[i], (s, zz * 2 + core))

    def second_cut(i):
        for side in (1, 0):
            (dev, b), (dev2, b2) = axes(side, up(i + 1))
            arrive(first_in[side].at[i], x_s.at[0, side, i], x_r.at[0, side, i], (dev, d))
            got = first_in[side][i, part(1 - b2), :].astype(f32)
            own = u_out[i, part(1 - b2), lanes(side, b)].astype(f32)
            mid_out[side][i] = (own + got).astype(bf16)
            go(
                mid_out[side].at[i], second_in[side].at[i],
                x_s.at[1, side, i], x_r.at[1, side, i], (dev2, d),
            )

    def z_step(i):
        zz = up(i + 1)
        for side in (1, 0):
            (_, b), (dev2, b2) = axes(side, zz)
            arrive(second_in[side].at[i], x_s.at[1, side, i], x_r.at[1, side, i], (dev2, d))
            total = u_out[i, part(b2), lanes(side, b)].astype(f32)
            total = total + first_in[side][i, part(b2), :].astype(f32)
            total = total + second_in[side][i].astype(f32)
            at = slice(offs[side], offs[side] + wide[side])
            if i < n_z - 1:
                z_out[i, :, at] = total.astype(bf16)
            else:
                z_own[:, at] = total
        if i < n_z - 1:
            go(z_out.at[i], z_in.at[i], z_s.at[i], z_r.at[i], (s, zz * 2 + core))

    halves = (slice(0, hr), slice(hr, 2 * hr))

    def tail_first():
        total = u_out[n_z - 1, :, tail].astype(f32)
        for i in range(n_z - 1):
            arrive(c_in.at[i], c_s.at[i], c_r.at[i], (s, down(i + 1) * 2 + core))
            total = total + c_in[i].astype(f32)
        c_own[0] = total.astype(bf16)
        for h in (0, 1):
            go(c_own.at[0, halves[h]], c_got.at[0, halves[h]], t_s.at[0, h], t_r.at[0, h], (seq_peer[1 + h], d))

    def tail_second():
        for h in (0, 1):
            arrive(c_got.at[0, halves[h]], t_s.at[0, h], t_r.at[0, h], (seq_peer[1 + h], d))
            total = c_own[0, halves[h]].astype(f32) + c_got[0, halves[h]].astype(f32)
            c_own[1, halves[h]] = total.astype(bf16)
            go(c_own.at[1, halves[h]], c_got.at[1, halves[h]], t_s.at[1, h], t_r.at[1, h], (seq_peer[2 - h], d))

    def tail_last():
        for h in (0, 1):
            arrive(c_got.at[1, halves[h]], t_s.at[1, h], t_r.at[1, h], (seq_peer[2 - h], d))
        total = c_own[1].astype(f32) + c_got[1].astype(f32)
        for b in range(2, n_bits):
            own = total.astype(bf16)
            c_own[b] = own
            dev = (flip(s, 1 << b), d)
            go(c_own.at[b], c_got.at[b], t_s.at[b, 0], t_r.at[b, 0], dev)
            arrive(c_got.at[b], t_s.at[b, 0], t_r.at[b, 0], dev)
            total = own.astype(f32) + c_got[b].astype(f32)
        wg_ref[:, tail] = total * scale

    def grad_norm(h):
        dn = mm(g_ref[...], w_full[hcols(h), :], 1, 1)
        u = attn[:, hcols(h)]
        da = (inv[h] * (dn - u * jnp.mean(dn * u, -1, keepdims=True))).astype(bf16)
        dattn[:, hcols(h)] = da
        s_out[1, 0, hcols(h)] = mm(q_ref[:, hcols(h)], da, 0, 0).astype(bf16)

    def parts(i):
        return range(i * n_z // CHUNKS, (i + 1) * n_z // CHUNKS)

    def offsets_of(i):
        if zb == 1:
            return [CHUNKS - 1 - i]
        return list(range(n_z)) if i == CHUNKS - 1 else []

    def rows_over(i):
        for k in offsets_of(i):
            if k == 0:
                continue
            src = down(k) * 2 + core
            arrive(w_full.at[brow(src), own_q[1]], w1_s.at[1, k - 1], w1_r.at[1, k - 1], (s, src))
            for j in (1, 2):
                arrive(
                    w_full.at[brow(src), qcols(seq_peer[j])], w2_s.at[j - 1, k - 1],
                    w2_r.at[j - 1, k - 1], (seq_peer[j], d),
                )
            go(w_full.at[brow(src)], w_full.at[brow(src)], w3_s.at[k], w3_r.at[k], (s, peer))

    def rows_here(i):
        for k in offsets_of(i):
            src = down(k) * 2 + 1 - core
            arrive(w_full.at[brow(src)], w3_s.at[k], w3_r.at[k], (s, peer))

    def cut_again(i):
        for j in parts(i):
            second_cut(j)

    def last_cut(i):
        for j in parts(i):
            z_step(j)

    def every(i, last):
        if zb == 1:
            return [i]
        return list(range(n_z)) if last else []

    def finish(i, last=False):
        for b in range(1, n_bits):
            state_step(0, b, i)
        prior[chunk(i)] = acc[chunk(i)].astype(bf16)
        acc[chunk(i)] = jnp.zeros((half, size), f32)
        heads_of(i, finish_attn)
        for j in every(i, last):
            swap_cores(j)

    def cut_first(i, last=False):
        for j in every(i, last):
            first_cut(j)

    finish(0)
    finish(1)
    cut_first(0)
    finish(2)
    cut_first(1)
    finish(3, True)
    cut_first(2)
    rows_over(2)
    rows_over(3)
    rows_here(3)
    first_state(1, 3, grad_norm)
    cut_first(3, True)
    rows_over(1)
    cut_again(0)
    rows_here(2)
    first_state(1, 2, grad_norm)
    rows_over(0)
    cut_again(1)
    rows_here(1)
    first_state(1, 1, grad_norm)
    cut_again(2)
    rows_here(0)
    first_state(1, 0, grad_norm)
    cut_again(3)

    def make_scores(h):
        ds = (mm(dattn[:, hcols(h)], v_ref[:, hcols(h)], 1, 1) * vis_ref[...]).astype(bf16)
        dsc[h] = ds
        qg = mm(ds, k_ref[:, hcols(h)], 1, 0) + mm(dattn[:, hcols(h)], prior[hcols(h), :], 1, 1)
        qg_ref[:, hcols(h)] = qg.astype(bf16)

    def make_out(h):
        out_ref[:, hcols(h)] = mm(normed[...], w_full[:, hcols(h)], 1, 0).astype(bf16)

    heads_of(3, make_scores)
    last_cut(0)
    state_step(1, 0, 3)
    heads_of(2, make_scores)
    last_cut(1)
    tail_first()
    state_step(1, 0, 2)
    heads_of(1, make_scores)
    last_cut(2)
    state_step(1, 0, 1)
    heads_of(0, make_scores)
    tail_second()
    last_cut(3)
    state_step(1, 0, 0)

    def local_grads(h):
        attn[:, hcols(h)] = mm(dsc[h], q_ref[:, hcols(h)], 0, 0)
        dnormed[:, hcols(h)] = mm(wts[h], dattn[:, hcols(h)], 0, 0)


    total = z_own[...]
    for i in range(n_z - 1):
        src = down(i + 1) * 2 + core
        arrive(z_in.at[i], z_s.at[i], z_r.at[i], (s, src))
        total = total + z_in[i].astype(f32)
    for b in range(2, n_bits):
        own = total.astype(bf16)
        r_out[b - 2] = own
        dev = (flip(s, 1 << b), d)
        go(r_out.at[b - 2], r_in.at[b - 2], r_s.at[b - 2], r_r.at[b - 2], dev)
        arrive(r_in.at[b - 2], r_s.at[b - 2], r_r.at[b - 2], dev)
        total = own.astype(f32) + r_in[b - 2].astype(f32)
    place = lax.rem(s, QUAD)
    f_all[place] = total.astype(bf16)
    for j in (3, 1, 2):
        go(f_all.at[place], f_all.at[place], f_s.at[j - 1], f_r.at[j - 1], (seq_peer[j], d))

    for i in range(CHUNKS):
        heads_of(i, make_out)
    for i in reversed(range(CHUNKS)):
        heads_of(i, local_grads)

    tail_last()

    def last_grads(h):
        kg = attn[:, hcols(h)] + mm(v_ref[:, hcols(h)], later[hcols(h), :], 1, 1)
        kg_ref[:, hcols(h)] = kg.astype(bf16)
        vg = dnormed[:, hcols(h)] + mm(k_ref[:, hcols(h)], later[hcols(h), :], 1, 0)
        vg_ref[:, hcols(h)] = vg.astype(bf16)

    for i in reversed(range(CHUNKS)):
        for b in range(1, n_bits):
            state_step(1, b, i)
        later[chunk(i)] = acc[chunk(i)].astype(bf16)
        heads_of(i, last_grads)

    for j in (1, 2, 3):
        there = lax.rem(seq_peer[j], QUAD)
        arrive(f_all.at[there], f_s.at[j - 1], f_r.at[j - 1], (seq_peer[j], d))
    for p in range(QUAD):
        for side in (0, 1):
            turn = lax.rem(z + side, 2) == 0
            b, b2 = jnp.where(turn, p % 2, p // 2), jnp.where(turn, p // 2, p % 2)
            got = f_all[p, :, offs[side]:offs[side] + wide[side]]
            wg_ref[part(b2), lanes(side, b)] = got.astype(f32) * scale
    for c, when in sent:
        if when is None:
            c.wait_send()
        else:
            pl.when(when)(c.wait_send)


def store(*refs):
    src, dst, sems = refs[:5], refs[5:10], refs[10]
    saves = [pltpu.make_async_copy(src[i], dst[i], sems.at[i]) for i in range(5)]
    for c in saves:
        c.start()
    for c in saves:
        c.wait()


def on_device(n_seq, n_dp, queries, keys, values, out_grad, out_weight, block_mask):
    _, tokens, width = queries.shape
    rows, cols = out_weight.shape
    size = width // H
    n_z = n_dp // 2
    n_bits = n_seq.bit_length() - 1
    more = max(n_bits - 2, 1)
    quarter = cols // QUAD
    eighth = quarter // 2
    kept = quarter + eighth
    half_rows = rows // 2
    dma = pltpu.SemaphoreType.DMA
    vm = pltpu.VMEM
    act = jax.ShapeDtypeStruct((tokens, width), bf16)
    spec = pl.BlockSpec(memory_space=pltpu.VMEM)
    outs = pl.pallas_call(
        functools.partial(kernel, n_seq, n_dp),
        out_shape=[vm((tokens, width), bf16)] * 4 + [vm((rows, cols), f32)],
        in_specs=[pl.BlockSpec(memory_space=pltpu.HBM)] * 6,
        out_specs=[spec] * 5,
        scratch_shapes=[
            vm((width, cols), bf16),
            vm((tokens, tokens), f32),
            vm((2, n_bits, width, size), bf16),
            vm((2, n_bits, width, size), bf16),
            vm((width, size), f32),
            vm((width, size), bf16),
            vm((width, size), bf16),
            vm((H, tokens, tokens), bf16),
            vm((tokens, width), f32),
            vm((H, tokens, 1), f32),
            vm((tokens, width), bf16),
            vm((tokens, width), f32),
            vm((tokens, width), bf16),
            vm((H, tokens, tokens), bf16),
            vm((width, cols), bf16),
            vm((n_z, rows, cols), bf16),
            vm((n_z, rows, cols), bf16),
            vm((n_z, rows, eighth), bf16), vm((n_z, rows, quarter), bf16),
            vm((n_z, half_rows, eighth), bf16), vm((n_z, half_rows, quarter), bf16),
            vm((n_z, half_rows, eighth), bf16), vm((n_z, half_rows, quarter), bf16),
            vm((n_z - 1, half_rows, kept), bf16),
            vm((n_z - 1, half_rows, kept), bf16),
            vm((half_rows, kept), f32),
            vm((n_z - 1, rows, quarter), bf16),
            vm((n_bits, rows, quarter), bf16),
            vm((n_bits, rows, quarter), bf16),
            vm((more, half_rows, kept), bf16),
            vm((more, half_rows, kept), bf16),
            vm((QUAD, half_rows, kept), bf16),
            dma((2, n_z - 1)), dma((2, n_z - 1)),
            dma((2, n_z - 1)), dma((2, n_z - 1)),
            dma((n_z,)), dma((n_z,)),
            dma((2, n_bits, H)), dma((2, n_bits, H)),
            dma((n_z,)), dma((n_z,)),
            dma((2, 2, n_z)), dma((2, 2, n_z)),
            dma((n_z - 1,)), dma((n_z - 1,)),
            dma((n_z - 1,)), dma((n_z - 1,)),
            dma((n_bits, 2)), dma((n_bits, 2)),
            dma((more,)), dma((more,)),
            dma((3,)), dma((3,)),
            vm((tokens, width), bf16), vm((tokens, width), bf16),
            vm((tokens, width), bf16), vm((tokens, width), bf16),
            vm(block_mask.shape[1:], jnp.int32), dma((6,)),
        ],
        compiler_params=pltpu.CompilerParams(
            collective_id=0, has_side_effects=True, vmem_limit_bytes=40 * 1024 * 1024
        ),
    )(*[pltpu.with_memory_space_constraint(a, pltpu.HBM) for a in (queries[0], keys[0], values[0], out_grad[0], out_weight, block_mask[0])])
    outs = pl.pallas_call(
        store,
        out_shape=[jax.ShapeDtypeStruct(o.shape, o.dtype) for o in outs],
        in_specs=[spec] * 5,
        out_specs=[pl.BlockSpec(memory_space=pltpu.HBM)] * 5,
        scratch_shapes=[dma((5,))],
        compiler_params=pltpu.CompilerParams(vmem_limit_bytes=4 * 1024 * 1024),
    )(*outs)
    return tuple(o[None] for o in outs[:4]) + (outs[4],)


def solution(mesh):
    token_spec = P("dp", "seq", None)
    row_spec = P("dp", None)
    return jax.shard_map(
        functools.partial(on_device, mesh.shape["seq"], mesh.shape["dp"]),
        mesh=mesh,
        in_specs=(token_spec,) * 4 + (row_spec, token_spec),
        out_specs=(token_spec,) * 4 + (row_spec,),
        check_vma=False,
    )
```

```python
import functools
import math

import jax
import jax.numpy as jnp
from jax import lax
from jax.experimental import pallas as pl
from jax.experimental.pallas import tpu as pltpu
from jax.sharding import PartitionSpec as P

H = 8
norm_eps = 1e-05
MESH = pl.DeviceIdType.MESH
f32 = jnp.float32
bf16 = jnp.bfloat16
QUAD = 4
CHUNKS = 4
UNROLL = 4


def bit(i, m):
    return lax.rem(lax.div(i, m), 2)


def flip(i, m):
    return i + m - 2 * m * bit(i, m)


def mm(a, b, da, db):
    return lax.dot_general(a, b, (((da,), (db,)), ((), ())), preferred_element_type=f32)


def over_heads(first, count, fn):
    def body(i, c):
        fn(first + i)
        return c

    lax.fori_loop(0, count, body, 0, unroll=min(UNROLL, count))


def visibility(mask, tokens):
    blocks = mask.shape[0]
    width = tokens // blocks
    t = lax.broadcasted_iota(jnp.int32, (tokens, blocks), 0)
    b = lax.broadcasted_iota(jnp.int32, (tokens, blocks), 1) * width
    member = jnp.where((t >= b) & (t < b + width), 1.0, 0.0)
    r = lax.broadcasted_iota(jnp.int32, (blocks, blocks), 0)
    c = lax.broadcasted_iota(jnp.int32, (blocks, blocks), 1)
    lower = jnp.where((mask == 1) & (c < r), 1.0, 0.0)
    member = member.astype(bf16)
    rows = mm(member, lower.astype(bf16), 1, 0).astype(bf16)
    earlier = mm(rows, member, 1, 1)
    same = mm(member, member, 1, 1)
    row = lax.broadcasted_iota(jnp.int32, (tokens, tokens), 0)
    col = lax.broadcasted_iota(jnp.int32, (tokens, tokens), 1)
    return earlier + jnp.where(col <= row, same, 0.0)


def kernel(
    n_seq, n_dp, q_hbm, k_hbm, v_hbm, g_hbm, w_ref, mask_hbm,
    out_ref, qg_ref, kg_ref, vg_ref, wg_ref,
    w_full, vis_ref, s_out, s_in, acc, prior, later, wts, attn, inv, normed,
    dnormed, dattn, dsc, term, a_in, u_out, *rest,
):
    first_in, mid_out, second_in, rest = rest[:2], rest[2:4], rest[4:6], rest[6:]
    z_out, z_in, z_own, c_in, c_own, c_got, r_out, r_in, f_all, *rest = rest
    w1_s, w1_r, w2_s, w2_r, w3_s, w3_r, st_s, st_r, a_s, a_r, x_s, x_r, z_s, z_r, *rest = rest
    c_s, c_r, t_s, t_r, r_s, r_r, f_s, f_r, q_ref, k_ref, v_ref, g_ref, mask_ref, in_s = rest
    tokens, width = q_ref.shape
    size = width // H
    n_z = n_dp // 2
    rows = w_ref.shape[0]
    cols = w_ref.shape[1]
    quarter = cols // QUAD
    eighth = quarter // 2
    hr = rows // 2
    scale = 1.0 / math.sqrt(n_seq * n_dp * tokens)
    n_bits = n_seq.bit_length() - 1
    s = lax.axis_index("seq")
    d = lax.axis_index("dp")
    z = lax.div(d, 2)
    core = lax.rem(d, 2)
    peer = flip(d, 1)
    seq_peer = {1: flip(s, 1), 2: flip(s, 2), 3: flip(flip(s, 1), 2)}
    bits = (bit(s, 1), bit(s, 2))
    zb = n_z // CHUNKS
    half = width // CHUNKS
    per = H // CHUNKS

    def qcols(seq_index):
        return pl.ds(pl.multiple_of(lax.rem(seq_index, QUAD) * quarter, quarter), quarter)

    def brow(dp_index):
        return pl.ds(pl.multiple_of(dp_index * rows, rows), rows)

    def hcols(h):
        return pl.ds(pl.multiple_of(h * size, size), size)

    def up(k):
        return lax.rem(z + k, n_z)

    def down(k):
        return lax.rem(z + n_z - k, n_z)

    def chunk_at(i):
        return lax.rem(lax.div(z, zb) + 1 + i, CHUNKS)

    def chunk(i):
        return pl.ds(pl.multiple_of(chunk_at(i) * half, half), half)

    def heads_of(i, fn):
        over_heads(chunk_at(i) * per, per, fn)

    def rc(src, dst, ss, rs, dev):
        return pltpu.make_async_remote_copy(
            src_ref=src, dst_ref=dst, send_sem=ss, recv_sem=rs, device_id=dev,
            device_id_type=MESH,
        )

    sent = []

    def go(*a, when=None):
        c = rc(*a)
        if when is None:
            c.start()
        else:
            pl.when(when)(c.start)
        sent.append((c, when))

    def arrive(dst, ss, rs, dev):
        rc(dst, dst, ss, rs, dev).wait_recv()

    loads = {}
    pairs = [(k_hbm, k_ref), (v_hbm, v_ref), (q_hbm, q_ref), (mask_hbm, mask_ref), (g_hbm, g_ref)]
    pairs.append((w_ref, w_full.at[brow(d)]))
    for i, name in enumerate("kvqmgw"):
        loads[name] = pltpu.make_async_copy(pairs[i][0], pairs[i][1], in_s.at[i])
        loads[name].start()

    barrier = pltpu.get_barrier_semaphore()
    partners = [(s, peer)]
    partners += [(seq_peer[j], d) for j in (1, 2, 3)]
    partners += [(flip(s, 1 << b), d) for b in range(2, n_bits)]
    partners += [(s, up(i) * 2 + core) for i in range(1, n_z)]
    for p in partners:
        pl.semaphore_signal(barrier, inc=1, device_id=p, device_id_type=MESH)
    acc[...] = jnp.zeros_like(acc)
    pl.semaphore_wait(barrier, len(partners))

    own_q = [qcols(s), qcols(seq_peer[3])]
    for qn in range(2):
        for i in range(1, n_z):
            go(
                w_ref.at[:, own_q[qn]], w_full.at[brow(d), own_q[qn]],
                w1_s.at[qn, i - 1], w1_r.at[qn, i - 1], (s, up(i) * 2 + core),
            )
    go(w_ref, w_full.at[brow(d)], w3_s.at[0], w3_r.at[0], (s, peer))
    loads["k"].wait()
    loads["v"].wait()

    def roles(way, b):
        own = bit(s, 1 << b)
        above = lax.div(s, 2 << b)
        last = (n_seq >> (b + 1)) - 1
        takes = own == 1 if way == 0 else own == 0
        if last == 0:
            return takes, None
        return takes, above != last if way == 0 else above != 0

    def head_rows(i, k):
        return hcols(chunk_at(i) * per + k)

    def send_state(way, b, i, k, when):
        go(
            s_out.at[way, b, head_rows(i, k)], s_in.at[way, b, head_rows(i, k)],
            st_s.at[way, b, i * per + k], st_r.at[way, b, i * per + k], (flip(s, 1 << b), d),
            when=when,
        )

    def first_state(way, i, fn):
        takes, more = roles(way, 0)
        gives = jnp.logical_not(takes)
        for k in range(per):
            over_heads(chunk_at(i) * per + k, 1, fn)
            send_state(way, 0, i, k, gives if more is None else jnp.logical_or(gives, more))

    def state_step(way, b, i):
        for k in range(per):
            head_step(way, b, i, k)

    def head_step(way, b, i, k):
        takes, more = roles(way, b)
        at = head_rows(i, k)

        def receive():
            arrive(
                s_in.at[way, b, at], st_s.at[way, b, i * per + k], st_r.at[way, b, i * per + k],
                (flip(s, 1 << b), d),
            )

        def pass_on():
            total = s_out[way, b, at].astype(f32) + s_in[way, b, at].astype(f32)
            s_out[way, b + 1, at] = total.astype(bf16)

        def take():
            acc[at] += s_in[way, b, at].astype(f32)

        if more is None:
            pl.when(takes)(receive)
        else:
            pl.when(jnp.logical_or(takes, more))(receive)
            pl.when(more)(pass_on)
            send_state(way, b + 1, i, k, more)
        pl.when(takes)(take)

    def make_state(h):
        st = mm(k_ref[:, hcols(h)], v_ref[:, hcols(h)], 0, 0)
        s_out[0, 0, hcols(h)] = st.astype(bf16)

    for i in (0, 1, 2, 3):
        first_state(0, i, make_state)

    loads["q"].wait()
    loads["m"].wait()
    vis_ref[...] = visibility(mask_ref[...], tokens)

    def local_attn(h):
        sc = mm(q_ref[:, hcols(h)], k_ref[:, hcols(h)], 1, 1)
        wt = (sc * vis_ref[...]).astype(bf16)
        wts[h] = wt
        attn[:, hcols(h)] = mm(wt, v_ref[:, hcols(h)], 1, 0)

    for i in (0, 1, 2, 3):
        heads_of(i, local_attn)

    for i in (0, 1, 2, 3):
        state_step(0, 0, i)

    for i in range(1, n_z):
        src = down(i) * 2 + core
        arrive(w_full.at[brow(src), own_q[0]], w1_s.at[0, i - 1], w1_r.at[0, i - 1], (s, src))
        for j in (1, 2):
            go(
                w_full.at[brow(src), own_q[0]], w_full.at[brow(src), own_q[0]],
                w2_s.at[j - 1, i - 1], w2_r.at[j - 1, i - 1], (seq_peer[j], d),
            )

    loads["g"].wait()
    loads["w"].wait()

    def finish_attn(h):
        a = attn[:, hcols(h)] + mm(q_ref[:, hcols(h)], prior[hcols(h), :], 1, 0)
        iv = lax.rsqrt(jnp.mean(a * a, -1, keepdims=True) + norm_eps)
        u = a * iv
        attn[:, hcols(h)] = u
        inv[h] = iv
        n = u.astype(bf16)
        normed[:, hcols(h)] = n
        term[hcols(h), :] = mm(n, g_ref[...], 0, 0).astype(bf16)

    starts = (0, quarter)
    wide = (eighth, quarter)
    offs = (0, eighth)
    tail = slice(3 * quarter, 4 * quarter)

    def axes(side, block):
        turn = lax.rem(block + side, 2) == 0
        first = jnp.where(turn, seq_peer[1], seq_peer[2]), jnp.where(turn, bits[0], bits[1])
        second = jnp.where(turn, seq_peer[2], seq_peer[1]), jnp.where(turn, bits[1], bits[0])
        return first, second

    def lanes(side, b):
        return pl.ds(pl.multiple_of(starts[side] + b * wide[side], eighth), wide[side])

    def part(b):
        return pl.ds(pl.multiple_of(b * hr, hr), hr)

    def swap_cores(i):
        zz = up(i + 1)
        go(term.at[brow(zz * 2 + 1 - core)], a_in.at[i], a_s.at[i], a_r.at[i], (s, peer))

    def first_cut(i):
        zz = up(i + 1)
        arrive(a_in.at[i], a_s.at[i], a_r.at[i], (s, peer))
        u_out[i] = (term[brow(zz * 2 + core), :].astype(f32) + a_in[i].astype(f32)).astype(bf16)
        for side in (1, 0):
            (dev, b), _ = axes(side, zz)
            go(
                u_out.at[i, :, lanes(side, 1 - b)], first_in[side].at[i],
                x_s.at[0, side, i], x_r.at[0, side, i], (dev, d),
            )
        if i < n_z - 1:
            go(u_out.at[i, :, tail], c_in.at[i], c_s.at[i], c_r.at[i], (s, zz * 2 + core))

    def second_cut(i):
        for side in (1, 0):
            (dev, b), (dev2, b2) = axes(side, up(i + 1))
            arrive(first_in[side].at[i], x_s.at[0, side, i], x_r.at[0, side, i], (dev, d))
            got = first_in[side][i, part(1 - b2), :].astype(f32)
            own = u_out[i, part(1 - b2), lanes(side, b)].astype(f32)
            mid_out[side][i] = (own + got).astype(bf16)
            go(
                mid_out[side].at[i], second_in[side].at[i],
                x_s.at[1, side, i], x_r.at[1, side, i], (dev2, d),
            )

    def z_step(i):
        zz = up(i + 1)
        for side in (1, 0):
            (_, b), (dev2, b2) = axes(side, zz)
            arrive(second_in[side].at[i], x_s.at[1, side, i], x_r.at[1, side, i], (dev2, d))
            total = u_out[i, part(b2), lanes(side, b)].astype(f32)
            total = total + first_in[side][i, part(b2), :].astype(f32)
            total = total + second_in[side][i].astype(f32)
            at = slice(offs[side], offs[side] + wide[side])
            if i < n_z - 1:
                z_out[i, :, at] = total.astype(bf16)
            else:
                z_own[:, at] = total
        if i < n_z - 1:
            go(z_out.at[i], z_in.at[i], z_s.at[i], z_r.at[i], (s, zz * 2 + core))

    halves = (slice(0, hr), slice(hr, 2 * hr))

    def tail_first():
        total = u_out[n_z - 1, :, tail].astype(f32)
        for i in range(n_z - 1):
            arrive(c_in.at[i], c_s.at[i], c_r.at[i], (s, down(i + 1) * 2 + core))
            total = total + c_in[i].astype(f32)
        c_own[0] = total.astype(bf16)
        for h in (0, 1):
            go(c_own.at[0, halves[h]], c_got.at[0, halves[h]], t_s.at[0, h], t_r.at[0, h], (seq_peer[1 + h], d))

    def tail_second():
        for h in (0, 1):
            arrive(c_got.at[0, halves[h]], t_s.at[0, h], t_r.at[0, h], (seq_peer[1 + h], d))
            total = c_own[0, halves[h]].astype(f32) + c_got[0, halves[h]].astype(f32)
            c_own[1, halves[h]] = total.astype(bf16)
            go(c_own.at[1, halves[h]], c_got.at[1, halves[h]], t_s.at[1, h], t_r.at[1, h], (seq_peer[2 - h], d))

    def tail_last():
        for h in (0, 1):
            arrive(c_got.at[1, halves[h]], t_s.at[1, h], t_r.at[1, h], (seq_peer[2 - h], d))
        total = c_own[1].astype(f32) + c_got[1].astype(f32)
        for b in range(2, n_bits):
            own = total.astype(bf16)
            c_own[b] = own
            dev = (flip(s, 1 << b), d)
            go(c_own.at[b], c_got.at[b], t_s.at[b, 0], t_r.at[b, 0], dev)
            arrive(c_got.at[b], t_s.at[b, 0], t_r.at[b, 0], dev)
            total = own.astype(f32) + c_got[b].astype(f32)
        wg_ref[:, tail] = total * scale

    def grad_norm(h):
        dn = mm(g_ref[...], w_full[hcols(h), :], 1, 1)
        u = attn[:, hcols(h)]
        da = (inv[h] * (dn - u * jnp.mean(dn * u, -1, keepdims=True))).astype(bf16)
        dattn[:, hcols(h)] = da
        s_out[1, 0, hcols(h)] = mm(q_ref[:, hcols(h)], da, 0, 0).astype(bf16)

    def parts(i):
        return range(i * n_z // CHUNKS, (i + 1) * n_z // CHUNKS)

    def offsets_of(i):
        if zb == 1:
            return [CHUNKS - 1 - i]
        return list(range(n_z)) if i == CHUNKS - 1 else []

    def rows_over(i):
        for k in offsets_of(i):
            if k == 0:
                continue
            src = down(k) * 2 + core
            arrive(w_full.at[brow(src), own_q[1]], w1_s.at[1, k - 1], w1_r.at[1, k - 1], (s, src))
            for j in (1, 2):
                arrive(
                    w_full.at[brow(src), qcols(seq_peer[j])], w2_s.at[j - 1, k - 1],
                    w2_r.at[j - 1, k - 1], (seq_peer[j], d),
                )
            go(w_full.at[brow(src)], w_full.at[brow(src)], w3_s.at[k], w3_r.at[k], (s, peer))

    def rows_here(i):
        for k in offsets_of(i):
            src = down(k) * 2 + 1 - core
            arrive(w_full.at[brow(src)], w3_s.at[k], w3_r.at[k], (s, peer))

    def cut_again(i):
        for j in parts(i):
            second_cut(j)

    def last_cut(i):
        for j in parts(i):
            z_step(j)

    def every(i, last):
        if zb == 1:
            return [i]
        return list(range(n_z)) if last else []

    def finish(i, last=False):
        for b in range(1, n_bits):
            state_step(0, b, i)
        prior[chunk(i)] = acc[chunk(i)].astype(bf16)
        acc[chunk(i)] = jnp.zeros((half, size), f32)
        heads_of(i, finish_attn)
        for j in every(i, last):
            swap_cores(j)

    def cut_first(i, last=False):
        for j in every(i, last):
            first_cut(j)

    finish(0)
    finish(1)
    cut_first(0)
    finish(2)
    cut_first(1)
    finish(3, True)
    cut_first(2)
    rows_over(2)
    rows_over(3)
    rows_here(3)
    first_state(1, 3, grad_norm)
    cut_first(3, True)
    rows_over(1)
    cut_again(0)
    rows_here(2)
    first_state(1, 2, grad_norm)
    rows_over(0)
    cut_again(1)
    rows_here(1)
    first_state(1, 1, grad_norm)
    cut_again(2)
    rows_here(0)
    first_state(1, 0, grad_norm)
    cut_again(3)

    def make_scores(h):
        ds = (mm(dattn[:, hcols(h)], v_ref[:, hcols(h)], 1, 1) * vis_ref[...]).astype(bf16)
        dsc[h] = ds
        qg = mm(ds, k_ref[:, hcols(h)], 1, 0) + mm(dattn[:, hcols(h)], prior[hcols(h), :], 1, 1)
        qg_ref[:, hcols(h)] = qg.astype(bf16)

    def make_out(h):
        out_ref[:, hcols(h)] = mm(normed[...], w_full[:, hcols(h)], 1, 0).astype(bf16)

    heads_of(3, make_scores)
    last_cut(0)
    tail_first()
    state_step(1, 0, 3)
    heads_of(2, make_scores)
    last_cut(1)
    state_step(1, 0, 2)
    heads_of(1, make_scores)
    last_cut(2)
    state_step(1, 0, 1)
    heads_of(0, make_scores)
    tail_second()
    last_cut(3)
    state_step(1, 0, 0)

    def local_grads(h):
        attn[:, hcols(h)] = mm(dsc[h], q_ref[:, hcols(h)], 0, 0)
        dnormed[:, hcols(h)] = mm(wts[h], dattn[:, hcols(h)], 0, 0)


    total = z_own[...]
    for i in range(n_z - 1):
        src = down(i + 1) * 2 + core
        arrive(z_in.at[i], z_s.at[i], z_r.at[i], (s, src))
        total = total + z_in[i].astype(f32)
    for b in range(2, n_bits):
        own = total.astype(bf16)
        r_out[b - 2] = own
        dev = (flip(s, 1 << b), d)
        go(r_out.at[b - 2], r_in.at[b - 2], r_s.at[b - 2], r_r.at[b - 2], dev)
        arrive(r_in.at[b - 2], r_s.at[b - 2], r_r.at[b - 2], dev)
        total = own.astype(f32) + r_in[b - 2].astype(f32)
    place = lax.rem(s, QUAD)
    f_all[place] = total.astype(bf16)
    for j in (3, 1, 2):
        go(f_all.at[place], f_all.at[place], f_s.at[j - 1], f_r.at[j - 1], (seq_peer[j], d))

    for i in range(CHUNKS):
        heads_of(i, make_out)
    for i in reversed(range(CHUNKS)):
        heads_of(i, local_grads)

    tail_last()

    def last_grads(h):
        kg = attn[:, hcols(h)] + mm(v_ref[:, hcols(h)], later[hcols(h), :], 1, 1)
        kg_ref[:, hcols(h)] = kg.astype(bf16)
        vg = dnormed[:, hcols(h)] + mm(k_ref[:, hcols(h)], later[hcols(h), :], 1, 0)
        vg_ref[:, hcols(h)] = vg.astype(bf16)

    for i in reversed(range(CHUNKS)):
        for b in range(1, n_bits):
            state_step(1, b, i)
        later[chunk(i)] = acc[chunk(i)].astype(bf16)
        heads_of(i, last_grads)

    for j in (1, 2, 3):
        there = lax.rem(seq_peer[j], QUAD)
        arrive(f_all.at[there], f_s.at[j - 1], f_r.at[j - 1], (seq_peer[j], d))
    for p in range(QUAD):
        for side in (0, 1):
            turn = lax.rem(z + side, 2) == 0
            b, b2 = jnp.where(turn, p % 2, p // 2), jnp.where(turn, p // 2, p % 2)
            got = f_all[p, :, offs[side]:offs[side] + wide[side]]
            wg_ref[part(b2), lanes(side, b)] = got.astype(f32) * scale
    for c, when in sent:
        if when is None:
            c.wait_send()
        else:
            pl.when(when)(c.wait_send)


def store(*refs):
    src, dst, sems = refs[:5], refs[5:10], refs[10]
    saves = [pltpu.make_async_copy(src[i], dst[i], sems.at[i]) for i in range(5)]
    for c in saves:
        c.start()
    for c in saves:
        c.wait()


def on_device(n_seq, n_dp, queries, keys, values, out_grad, out_weight, block_mask):
    _, tokens, width = queries.shape
    rows, cols = out_weight.shape
    size = width // H
    n_z = n_dp // 2
    n_bits = n_seq.bit_length() - 1
    more = max(n_bits - 2, 1)
    quarter = cols // QUAD
    eighth = quarter // 2
    kept = quarter + eighth
    half_rows = rows // 2
    dma = pltpu.SemaphoreType.DMA
    vm = pltpu.VMEM
    act = jax.ShapeDtypeStruct((tokens, width), bf16)
    spec = pl.BlockSpec(memory_space=pltpu.VMEM)
    outs = pl.pallas_call(
        functools.partial(kernel, n_seq, n_dp),
        out_shape=[vm((tokens, width), bf16)] * 4 + [vm((rows, cols), f32)],
        in_specs=[pl.BlockSpec(memory_space=pltpu.HBM)] * 6,
        out_specs=[spec] * 5,
        scratch_shapes=[
            vm((width, cols), bf16),
            vm((tokens, tokens), f32),
            vm((2, n_bits, width, size), bf16),
            vm((2, n_bits, width, size), bf16),
            vm((width, size), f32),
            vm((width, size), bf16),
            vm((width, size), bf16),
            vm((H, tokens, tokens), bf16),
            vm((tokens, width), f32),
            vm((H, tokens, 1), f32),
            vm((tokens, width), bf16),
            vm((tokens, width), f32),
            vm((tokens, width), bf16),
            vm((H, tokens, tokens), bf16),
            vm((width, cols), bf16),
            vm((n_z, rows, cols), bf16),
            vm((n_z, rows, cols), bf16),
            vm((n_z, rows, eighth), bf16), vm((n_z, rows, quarter), bf16),
            vm((n_z, half_rows, eighth), bf16), vm((n_z, half_rows, quarter), bf16),
            vm((n_z, half_rows, eighth), bf16), vm((n_z, half_rows, quarter), bf16),
            vm((n_z - 1, half_rows, kept), bf16),
            vm((n_z - 1, half_rows, kept), bf16),
            vm((half_rows, kept), f32),
            vm((n_z - 1, rows, quarter), bf16),
            vm((n_bits, rows, quarter), bf16),
            vm((n_bits, rows, quarter), bf16),
            vm((more, half_rows, kept), bf16),
            vm((more, half_rows, kept), bf16),
            vm((QUAD, half_rows, kept), bf16),
            dma((2, n_z - 1)), dma((2, n_z - 1)),
            dma((2, n_z - 1)), dma((2, n_z - 1)),
            dma((n_z,)), dma((n_z,)),
            dma((2, n_bits, H)), dma((2, n_bits, H)),
            dma((n_z,)), dma((n_z,)),
            dma((2, 2, n_z)), dma((2, 2, n_z)),
            dma((n_z - 1,)), dma((n_z - 1,)),
            dma((n_z - 1,)), dma((n_z - 1,)),
            dma((n_bits, 2)), dma((n_bits, 2)),
            dma((more,)), dma((more,)),
            dma((3,)), dma((3,)),
            vm((tokens, width), bf16), vm((tokens, width), bf16),
            vm((tokens, width), bf16), vm((tokens, width), bf16),
            vm(block_mask.shape[1:], jnp.int32), dma((6,)),
        ],
        compiler_params=pltpu.CompilerParams(
            collective_id=0, has_side_effects=True, vmem_limit_bytes=40 * 1024 * 1024
        ),
    )(*[pltpu.with_memory_space_constraint(a, pltpu.HBM) for a in (queries[0], keys[0], values[0], out_grad[0], out_weight, block_mask[0])])
    outs = pl.pallas_call(
        store,
        out_shape=[jax.ShapeDtypeStruct(o.shape, o.dtype) for o in outs],
        in_specs=[spec] * 5,
        out_specs=[pl.BlockSpec(memory_space=pltpu.HBM)] * 5,
        scratch_shapes=[dma((5,))],
        compiler_params=pltpu.CompilerParams(vmem_limit_bytes=4 * 1024 * 1024),
    )(*outs)
    return tuple(o[None] for o in outs[:4]) + (outs[4],)


def solution(mesh):
    token_spec = P("dp", "seq", None)
    row_spec = P("dp", None)
    return jax.shard_map(
        functools.partial(on_device, mesh.shape["seq"], mesh.shape["dp"]),
        mesh=mesh,
        in_specs=(token_spec,) * 4 + (row_spec, token_spec),
        out_specs=(token_spec,) * 4 + (row_spec,),
        check_vma=False,
    )
```
